256 devices in a mesh: clip: 64 (over x, z, core), slab: 4 (over y).
Axes of the slice: x: 4, y: 4, z: 8, core: 2. Of those that a mesh axis runs over, the one named last changes fastest.
Arguments:
- frames_in: bfloat16 [128, 16, 128, 128], P('clip', 'slab')
- clip_ids: int32 [64], replicated, may hold values from 0 to 15, never falling along the last dimension, each value on 1 to 32 neighbouring positions
- gain_one: float32 [128], replicated, may hold values from 0.25 to 1.75
- shift_one: float32 [128], replicated, may hold values from -3 to 3
- kernel_one: bfloat16 [3, 3, 3, 128, 128], replicated, may hold values from -0.109375 to 0.109375
- bias_one: float32 [128], replicated, may hold values from -3 to 3
- gain_two: float32 [128], replicated, may hold values from 0.25 to 1.75
- shift_two: float32 [128], replicated, may hold values from -3 to 3
- kernel_two: bfloat16 [3, 3, 3, 128, 128], replicated, may hold values from -0.109375 to 0.109375
- bias_two: float32 [128], replicated, may hold values from -3 to 3
Outputs:
- frames_out: bfloat16 [128, 16, 128, 128], P('clip', 'slab')
The draws below stay inside these ranges and needn't reach their ends.
Inputs may be any that keep to these rules, and one draw needn't show every extreme that they name: `clip_ids`: never falling along the blocks; each clip covers 1 to 32 blocks, one exactly 32.
All inputs are finite; a program needn't handle non-finite values.
Results may differ from the reference program's by a relative error of at most 0.0075.
Values may be sent and summed in bfloat16 or wider, within the bound.
A program may use at most 64 MiB of HBM per device.

```python
import math
import jax
import jax.numpy as jnp
import numpy as np
from jax import lax

C = 128
G = 32
FR_DEV = 2
ROWS = 4
W = 128
FRAMES = 128
HEIGHT = 16
CLIPS = 16
MOST = 32
N_CLIP = 64
N_SLAB = 4


def draw_frames_in(key, part):
    key_base, key_chan, key_cell, key_frame, key_row = jax.random.split(key, 5)
    shape = (FRAMES, HEIGHT, W, C)
    base = jax.random.normal(key_base, shape, jnp.float32)
    frame_order = jax.random.permutation(key_frame, FRAMES).astype(jnp.float32)
    frame_scale = 0.5 * jnp.exp(frame_order / max(FRAMES - 1, 1) * jnp.log(3.0))
    row_order = jax.random.permutation(key_row, HEIGHT).astype(jnp.float32)
    row_scale = 0.5 * jnp.exp(row_order / max(HEIGHT - 1, 1) * jnp.log(3.0))
    chan_scale = jnp.exp(jax.random.uniform(key_chan, (C,), jnp.float32, jnp.log(0.7), jnp.log(1.2)))
    cell_scale = jax.random.uniform(key_cell, (FRAMES, HEIGHT, W, 1), jnp.float32, 0.8, 1.2)
    return (base * frame_scale[:, None, None, None] * row_scale[None, :, None, None] * chan_scale * cell_scale).astype(jnp.bfloat16)


def split_up(number_of, total, most, lean):
    portions = [(1 << 20) // math.isqrt(standing ** lean) + 1 for standing in range(2, number_of + 1)]
    surplus, holding = total - most - (number_of - 1), [1] * (number_of - 1)
    while surplus > 0:
        movable = [i for i in range(number_of - 1) if holding[i] < most]
        mass, remaining = sum([portions[i] for i in movable]), surplus
        for i in movable:
            more = min(most - holding[i], max(1, remaining * portions[i] // mass), surplus)
            holding[i] = holding[i] + more
            surplus = surplus - more
    return np.array([most] + holding)


def ragged(own_key, number_of, total, reach, slope):
    if number_of == 2:
        one = jax.random.randint(own_key, (), max(1, total - reach), min(reach, total - 1) + 1)
        return jnp.stack([one, total - one])
    sizes = jnp.asarray(split_up(number_of, total, reach, slope), jnp.int32)
    couples = (number_of - 1) // 2
    source_of, sink = sizes[1:1 + 2 * couples:2], sizes[2:2 + 2 * couples:2]
    slack = jnp.minimum(source_of - 1, reach - sink)
    shifted = jax.random.randint(jax.random.fold_in(own_key, 1), (couples,), 0, 1 << 20) % (slack + 1)
    sizes = sizes.at[1:1 + 2 * couples:2].set(source_of - shifted).at[2:2 + 2 * couples:2].set(sink + shifted)
    return sizes[jax.random.permutation(jax.random.fold_in(own_key, 2), number_of)]


def gaussian(key, extent, scale, most, kind=jnp.bfloat16):
    result = scale * jax.random.normal(key, extent, jnp.float32)
    return jnp.clip(result, min=-most, max=most).astype(kind)


def setup_inputs(seed: int = 0) -> dict:
    key_of = jax.random.split(jax.random.key(seed), 11)
    return {
        "frames_in": draw_frames_in(jax.random.fold_in(key_of[10], 71), 0),
        "clip_ids": jnp.searchsorted(jnp.cumsum(ragged(key_of[1], CLIPS, N_CLIP, MOST, 2)), jnp.arange(N_CLIP), side="right").astype(jnp.int32),
        "gain_one": jnp.clip(1.0 + 0.15 * jax.random.normal(key_of[2], (C,), jnp.float32), 0.25, 1.75),
        "shift_one": gaussian(key_of[3], (C,), 0.5, 3.0, jnp.float32),
        "kernel_one": gaussian(key_of[4], (3, 3, 3, C, C), (27 * C) ** -0.5, 0.109375),
        "bias_one": gaussian(key_of[5], (C,), 0.5, 3.0, jnp.float32),
        "gain_two": jnp.clip(1.0 + 0.15 * jax.random.normal(key_of[6], (C,), jnp.float32), 0.25, 1.75),
        "shift_two": gaussian(key_of[7], (C,), 0.5, 3.0, jnp.float32),
        "kernel_two": gaussian(key_of[8], (3, 3, 3, C, C), (27 * C) ** -0.5, 0.109375),
        "bias_two": gaussian(key_of[9], (C,), 0.5, 3.0, jnp.float32),
    }


def group_act(values, frame_clip, gain, shift):
    floats = values.astype(jnp.float32)
    first = lax.optimization_barrier(jnp.sum(floats, axis=(1, 2)))
    second = lax.optimization_barrier(jnp.sum(floats * floats, axis=(1, 2)))
    onehot = (frame_clip[:, None] == jnp.arange(N_CLIP, dtype=jnp.int32)[None, :]).astype(jnp.float32)
    clip_first = jnp.dot(onehot.T, first, precision=lax.Precision.HIGHEST).reshape(N_CLIP, G, C // G).sum(2)
    clip_second = jnp.dot(onehot.T, second, precision=lax.Precision.HIGHEST).reshape(N_CLIP, G, C // G).sum(2)
    counts = jnp.maximum(lax.optimization_barrier(jnp.sum(onehot, axis=0)), 1.0) * (ROWS * N_SLAB * W * (C // G))
    mean = clip_first / counts[:, None]
    spread = clip_second / counts[:, None] - mean * mean
    inverse = lax.rsqrt(spread + 1e-06)
    mean_frame = jnp.repeat(jnp.dot(onehot, mean, precision=lax.Precision.HIGHEST), C // G, axis=1)
    inv_frame = jnp.repeat(jnp.dot(onehot, inverse, precision=lax.Precision.HIGHEST), C // G, axis=1)
    normed = (floats - mean_frame[:, None, None, :]) * inv_frame[:, None, None, :] * gain + shift
    return jax.nn.silu(normed).astype(jnp.bfloat16)

def convolve(act, frame_clip, kernel, bias):
    total_frames = act.shape[0]
    height = act.shape[1]
    width = act.shape[2]
    total = jnp.zeros((total_frames * height * width, C), jnp.float32)
    for back in range(3):
        moved = jnp.concatenate([jnp.zeros((back,) + act.shape[1:], act.dtype), act[:total_frames - back]], 0)
        valid = jnp.concatenate([jnp.zeros((back,), jnp.bool_), frame_clip[back:] == frame_clip[:total_frames - back]], 0)
        moved = moved * valid.astype(jnp.bfloat16)[:, None, None, None]
        padded = jnp.pad(moved, ((0, 0), (1, 1), (1, 1), (0, 0)))
        for row_off in range(3):
            for col_off in range(3):
                window = padded[:, row_off:row_off + height, col_off:col_off + width].reshape(-1, C)
                total = total + jnp.dot(window, kernel[2 - back, row_off, col_off], preferred_element_type=jnp.float32)
    return total.reshape(act.shape) + bias

def reference(frames_in, clip_ids, gain_one, shift_one, kernel_one, bias_one, gain_two, shift_two, kernel_two, bias_two):
    frame_clip = jnp.repeat(clip_ids, FR_DEV).astype(jnp.int32)
    act_one = group_act(frames_in, frame_clip, gain_one, shift_one)
    hidden = convolve(act_one, frame_clip, kernel_one, bias_one).astype(jnp.bfloat16)
    act_two = group_act(hidden, frame_clip, gain_two, shift_two)
    branch = convolve(act_two, frame_clip, kernel_two, bias_two)
    return (frames_in.astype(jnp.float32) + branch).astype(jnp.bfloat16)
```

```python
import functools

import jax
import jax.numpy as jnp
from jax import lax
from jax.experimental import pallas as pl
from jax.experimental.pallas import tpu as pltpu
from jax.sharding import PartitionSpec as P

MESH = pl.DeviceIdType.MESH
NX, NZ, NC, NY = 4, 8, 2, 4
CH = 128
W = 128
EPS = 1e-06


def hops(dx, dz, dy):
    return min(dx, NX - dx) + min(dz, NZ - dz) + min(dy, NY - dy)


NEAR = sorted(
    [(dy, dc) for dy in range(NY) for dc in range(NC) if dy or dc],
    key=lambda o: -hops(0, 0, o[0]),
)
FAR = sorted(
    [(dx, dz) for dx in range(NX) for dz in range(NZ) if dx or dz],
    key=lambda o: -hops(o[0], o[1], 0),
)


def kernel(
    x_hbm, ids_hbm, g1, s1, k1, b1, g2, s2, k2, b2, out_ref,
    xbuf, hbuf, act, wts, pbuf, ids, vecs, near, far, mask,
    load_sem, w_sem, halo_send, halo_recv, st_send, st_recv,
):
    clip = lax.axis_index("clip")
    y = lax.axis_index("slab")
    cx = clip // (NZ * NC)
    cz = (clip // NC) % NZ
    cc = clip % NC
    clips = NX * NZ * NC

    def near_dev(o):
        return (clip - cc + (cc + o[1]) % NC, (y + o[0]) % NY)

    def far_dev(o):
        return (((cx + o[0]) % NX) * (NZ * NC) + ((cz + o[1]) % NZ) * NC + cc, y)

    nxt, prv = (clip + 1) % clips, (clip + clips - 1) % clips
    up, down = (y + 1) % NY, (y + NY - 1) % NY
    halo_peers = [(nxt, y), (nxt, up), (nxt, down), (prv, y), (prv, up), (prv, down)]

    barrier = pltpu.get_barrier_semaphore()
    n_signals = 0
    for dev in [far_dev(o) for o in FAR] + halo_peers + [near_dev(o) for o in NEAR]:
        pl.semaphore_signal(barrier, inc=1, device_id=dev, device_id_type=MESH)
        n_signals += 1

    loads = [pltpu.make_async_copy(x_hbm, xbuf.at[pl.ds(2, 2), pl.ds(1, 4)], load_sem.at[0])]
    loads.append(pltpu.make_async_copy(ids_hbm, ids, load_sem.at[1]))
    for n, v in enumerate((g1, s1, b1, g2, s2, b2)):
        loads.append(pltpu.make_async_copy(v, vecs.at[n], load_sem.at[2 + n]))
    for cp in loads:
        cp.start()
    w_loads = []
    for cv, k in enumerate((k1, k2)):
        for dt in range(3):
            for dx in range(3):
                for i in range(2):
                    j = dt + i
                    cp = pltpu.make_async_copy(
                        k.at[dt, :, dx],
                        wts.at[cv, dx, :, pl.ds(j * CH, CH), pl.ds(i * CH, CH)],
                        w_sem.at[cv, len(w_loads) % 18],
                    )
                    cp.start()
                    w_loads.append(cp)

    def stats_of(rows):
        s = jnp.zeros((8, CH), jnp.float32)
        q = jnp.zeros((8, CH), jnp.float32)
        for v in rows:
            v = v.reshape(W // 8, 8, CH)
            s = s + jnp.sum(v, axis=0)
            q = q + jnp.sum(v * v, axis=0)
        return s, q

    def packed(s, q):
        return jnp.concatenate(
            [jnp.sum(s, axis=0, keepdims=True), jnp.sum(q, axis=0, keepdims=True)], axis=0
        )

    loads[0].wait()
    s, q = stats_of(
        xbuf[2 + f, 1 + r].astype(jnp.float32) for f in range(2) for r in range(4)
    )
    me_near = y * NC + cc
    me_far = cx * NZ + cz
    near[0, me_near] = packed(s, q)

    pl.semaphore_wait(barrier, n_signals)

    def near_sends(ar):
        cps = []
        for o in NEAR:
            cp = pltpu.make_async_remote_copy(
                src_ref=near.at[ar, me_near], dst_ref=near.at[ar, me_near],
                send_sem=st_send.at[ar, 0], recv_sem=st_recv.at[ar, 0],
                device_id=near_dev(o), device_id_type=MESH,
            )
            cp.start()
            cps.append(cp)
        return cps

    def far_sends(ar):
        cps = []
        for o in FAR:
            cp = pltpu.make_async_remote_copy(
                src_ref=far.at[ar, me_far], dst_ref=far.at[ar, me_far],
                send_sem=st_send.at[ar, 1], recv_sem=st_recv.at[ar, 1],
                device_id=far_dev(o), device_id_type=MESH,
            )
            cp.start()
            cps.append(cp)
        return cps

    def halo_sends(buf, n):
        own = buf.at[pl.ds(2, 2), pl.ds(1, 4)]
        first = buf.at[pl.ds(2, 2), 1]
        last = buf.at[pl.ds(2, 2), 4]
        plan = [
            (own, buf.at[pl.ds(0, 2), pl.ds(1, 4)], (nxt, y)),
            (last, buf.at[pl.ds(0, 2), 0], (nxt, up)),
            (first, buf.at[pl.ds(0, 2), 5], (nxt, down)),
            (last, buf.at[pl.ds(2, 2), 0], (clip, up)),
            (first, buf.at[pl.ds(2, 2), 5], (clip, down)),
        ]
        cps = []
        for m, (src, dst, dev) in enumerate(plan):
            cp = pltpu.make_async_remote_copy(
                src_ref=src, dst_ref=dst, send_sem=halo_send.at[n, m],
                recv_sem=halo_recv.at[n, m], device_id=dev, device_id_type=MESH,
            )
            cp.start()
            cps.append(cp)
        return cps

    def wait_near(ar):
        got = near.at[ar, pl.ds(0, len(NEAR))]
        pltpu.make_async_copy(got, got, st_recv.at[ar, 0]).wait()

    def wait_far(ar):
        got = far.at[ar, pl.ds(0, len(FAR))]
        pltpu.make_async_copy(got, got, st_recv.at[ar, 1]).wait()

    def fold(ar):
        for c in range(NC):
            t = near[ar, c]
            for k in range(1, NY):
                t = t + near[ar, k * NC + c]
            far[ar, me_far, 2 * c : 2 * c + 2, :] = t

    near_1 = near_sends(0)
    halo_1 = halo_sends(xbuf, 0)

    for cp in loads[1:]:
        cp.wait()
    own_id = ids[clip]
    blocks = jnp.float32(0)
    for k in range(NX * NZ):
        for c in range(NC):
            m = jnp.where(ids[k * NC + c] == own_id, jnp.float32(1), jnp.float32(0))
            blocks = blocks + m
            mask[k, 2 * c : 2 * c + 2, :] = jnp.full((2, CH), m, jnp.float32)
    prior_id = ids[jnp.maximum(clip - 1, 0)]
    same = jnp.where(prior_id == own_id, jnp.float32(1), jnp.float32(0))
    same = same * jnp.where(clip > 0, jnp.float32(1), jnp.float32(0))
    top = jnp.where(y > 0, jnp.float32(1), jnp.float32(0))
    bottom = jnp.where(y < NY - 1, jnp.float32(1), jnp.float32(0))
    one_count = 1.0 / (jnp.full((1, CH), blocks, jnp.float32) * (2 * 4 * NY * W * 4))
    zero = jnp.zeros((CH, CH), jnp.bfloat16)
    for cv in range(2):
        for dx in range(3):
            for dy in range(3):
                wts[cv, dx, dy, 0:CH, CH : 2 * CH] = zero
                wts[cv, dx, dy, 3 * CH : 4 * CH, 0:CH] = zero
    lane = lax.broadcasted_iota(jnp.int32, (2, CH), 1)

    def finish(ar, gain, shift):
        acc = jnp.zeros((4, CH), jnp.float32)
        for k in range(NX * NZ):
            acc = acc + far[ar, k] * mask[k]
        t = acc[0:2] + acc[2:4]
        t = t + jnp.where(lane % 2 == 0, pltpu.roll(t, CH - 1, 1), pltpu.roll(t, 1, 1))
        t = t + jnp.where(lane % 4 < 2, pltpu.roll(t, CH - 2, 1), pltpu.roll(t, 2, 1))
        mean = t[0:1] * one_count
        spread = t[1:2] * one_count - mean * mean
        inverse = lax.rsqrt(spread + EPS)
        scale = inverse * gain
        return 0.5 * scale, 0.5 * (shift - mean * scale)

    def activate(buf, scale, offset):
        for r in range(6):
            row = top if r == 0 else bottom if r == 5 else None
            for j in range(4):
                keep = row
                if j < 2:
                    keep = same if row is None else same * row
                sc, of = (scale, offset) if keep is None else (scale * keep, offset * keep)
                h = buf[j, r].astype(jnp.float32) * sc + of
                v = h + h * jnp.tanh(h)
                act[r * W : (r + 1) * W, j * CH : (j + 1) * CH] = v.astype(jnp.bfloat16)

    def convolve(cv):
        lhs = jnp.concatenate([act[d * W : (d + 4) * W, :] for d in range(3)], axis=1)
        for dx in range(3):
            rhs = wts[cv, dx].reshape(3 * 4 * CH, 2 * CH)
            pbuf[dx] = jnp.dot(lhs, rhs, preferred_element_type=jnp.float32)

    col = lax.broadcasted_iota(jnp.int32, (W, CH), 0)

    def joined(f, r, bias):
        at = (slice(r * W, (r + 1) * W), slice(f * CH, (f + 1) * CH))
        left = jnp.where(col == 0, 0.0, pltpu.roll(pbuf[(0, *at)], 1, 0))
        right = jnp.where(col == W - 1, 0.0, pltpu.roll(pbuf[(2, *at)], W - 1, 0))
        return (left + pbuf[(1, *at)]) + (right + bias)

    wait_near(0)
    fold(0)
    far_1 = far_sends(0)
    for cp in w_loads:
        cp.wait()
    for cp in halo_1:
        cp.wait_recv()
    wait_far(0)
    scale, offset = finish(0, vecs[0], vecs[1])
    activate(xbuf, scale, offset)
    convolve(0)

    def hidden_rows():
        for f in range(2):
            for r in range(4):
                v = joined(f, r, vecs[2]).astype(jnp.bfloat16)
                hbuf[2 + f, 1 + r] = v
                yield v.astype(jnp.float32)

    s, q = stats_of(hidden_rows())
    near[1, me_near] = packed(s, q)
    near_2 = near_sends(1)
    halo_2 = halo_sends(hbuf, 1)
    wait_near(1)
    fold(1)
    far_2 = far_sends(1)
    for cp in halo_2:
        cp.wait_recv()
    wait_far(1)
    scale, offset = finish(1, vecs[3], vecs[4])
    activate(hbuf, scale, offset)
    convolve(1)
    for f in range(2):
        for r in range(4):
            v = joined(f, r, vecs[5]) + xbuf[2 + f, 1 + r].astype(jnp.float32)
            out_ref[f, r] = v.astype(jnp.bfloat16)
    for cp in near_1 + near_2 + far_1 + far_2 + halo_1 + halo_2:
        cp.wait_send()


def per_device(x, ids, g1, s1, k1, b1, g2, s2, k2, b2):
    vec = [v.reshape(1, CH) for v in (g1, s1, b1, g2, s2, b2)]
    g1, s1, b1, g2, s2, b2 = vec
    anywhere = pl.BlockSpec(memory_space=pl.ANY)
    operands = [
        pltpu.with_memory_space_constraint(v, pltpu.HBM)
        for v in (x, ids, g1, s1, k1, b1, g2, s2, k2, b2)
    ]
    bf16, f32 = jnp.bfloat16, jnp.float32
    return pl.pallas_call(
        kernel,
        out_shape=jax.ShapeDtypeStruct(x.shape, bf16),
        in_specs=[anywhere] * 10,
        out_specs=pl.BlockSpec(memory_space=pltpu.VMEM),
        scratch_shapes=[
            pltpu.VMEM((4, 6, W, CH), bf16),
            pltpu.VMEM((4, 6, W, CH), bf16),
            pltpu.VMEM((6 * W, 4 * CH), bf16),
            pltpu.VMEM((2, 3, 3, 4 * CH, 2 * CH), bf16),
            pltpu.VMEM((3, 4 * W, 2 * CH), f32),
            pltpu.SMEM((64,), jnp.int32),
            pltpu.VMEM((6, 1, CH), f32),
            pltpu.VMEM((2, NY * NC, 2, CH), f32),
            pltpu.VMEM((2, NX * NZ, 4, CH), f32),
            pltpu.VMEM((NX * NZ, 4, CH), f32),
            pltpu.SemaphoreType.DMA((8,)),
            pltpu.SemaphoreType.DMA((2, 18)),
            pltpu.SemaphoreType.DMA((2, 5)),
            pltpu.SemaphoreType.DMA((2, 5)),
            pltpu.SemaphoreType.DMA((2, 2)),
            pltpu.SemaphoreType.DMA((2, 2)),
        ],
        compiler_params=pltpu.CompilerParams(
            collective_id=0, has_side_effects=True, vmem_limit_bytes=48 * 1024 * 1024
        ),
        cost_estimate=pl.CostEstimate(
            flops=4 * 1024 * 27 * CH * CH, bytes_accessed=2500000, transcendentals=800000
        ),
    )(*operands)


def solution(mesh):
    placed = (P("clip", "slab", None, None), P(), P(), P(), P(), P(), P(), P(), P(), P())
    return jax.shard_map(
        per_device,
        mesh=mesh,
        in_specs=placed,
        out_specs=P("clip", "slab", None, None),
        check_vma=False,
    )
```

```python
import functools

import jax
import jax.numpy as jnp
from jax import lax
from jax.experimental import pallas as pl
from jax.experimental.pallas import tpu as pltpu
from jax.sharding import PartitionSpec as P

MESH = pl.DeviceIdType.MESH
NX, NZ, NC, NY = 4, 8, 2, 4
CH = 128
W = 128
EPS = 1e-06


def hops(dx, dz, dy):
    return min(dx, NX - dx) + min(dz, NZ - dz) + min(dy, NY - dy)


def offsets(nx, ny, nz, nc):
    every = [
        (dx, dy, dz, dc)
        for dx in range(nx) for dy in range(ny) for dz in range(nz) for dc in range(nc)
    ]
    return sorted(every[1:], key=lambda o: -hops(o[0], o[2], o[1]))


PLANE = offsets(NX, NY, 1, 1)
LINE = offsets(1, 1, NZ, NC)
EVERY = offsets(NX, NY, NZ, NC)
AHEAD = sum(hops(o[0], o[2], o[1]) > 3 for o in EVERY)


def kernel(
    x_hbm, ids_hbm, g1, s1, k1, b1, g2, s2, k2, b2, out_ref,
    xbuf, hbuf, act, wts, pbuf, ids, vecs, plane, line, every, line_mask, mask,
    load_sem, w_sem, halo_send, halo_recv, st_send, st_recv,
):
    clip = lax.axis_index("clip")
    y = lax.axis_index("slab")
    cx = clip // (NZ * NC)
    cz = (clip // NC) % NZ
    cc = clip % NC
    clips = NX * NZ * NC

    def device(o):
        dx, dy, dz, dc = o
        at = (cx + dx) % NX if dx else cx
        at = at * NZ + ((cz + dz) % NZ if dz else cz)
        at = at * NC + ((cc + dc) % NC if dc else cc)
        return (at, (y + dy) % NY if dy else y)

    nxt, prv = (clip + 1) % clips, (clip + clips - 1) % clips
    up, down = (y + 1) % NY, (y + NY - 1) % NY
    halo_peers = [(nxt, y), (nxt, up), (nxt, down), (prv, y), (prv, up), (prv, down)]

    barrier = pltpu.get_barrier_semaphore()
    n_signals = 0
    for dev in [device(o) for o in PLANE + LINE] + halo_peers:
        pl.semaphore_signal(barrier, inc=1, device_id=dev, device_id_type=MESH)
        n_signals += 1

    loads = [pltpu.make_async_copy(x_hbm, xbuf.at[pl.ds(2, 2), pl.ds(1, 4)], load_sem.at[0])]
    loads.append(pltpu.make_async_copy(ids_hbm, ids, load_sem.at[1]))
    for n, v in enumerate((g1, s1, b1, g2, s2, b2)):
        loads.append(pltpu.make_async_copy(v, vecs.at[n], load_sem.at[2 + n]))
    for cp in loads:
        cp.start()
    w_loads = []
    for cv, k in enumerate((k1, k2)):
        for dt in range(3):
            for dx in range(3):
                for i in range(2):
                    j = dt + i
                    cp = pltpu.make_async_copy(
                        k.at[dt, :, dx],
                        wts.at[cv, dx, :, pl.ds(j * CH, CH), pl.ds(i * CH, CH)],
                        w_sem.at[cv, len(w_loads) % 18],
                    )
                    cp.start()
                    w_loads.append(cp)

    def stats_of(rows):
        s = jnp.zeros((8, CH), jnp.float32)
        q = jnp.zeros((8, CH), jnp.float32)
        for v in rows:
            v = v.reshape(W // 8, 8, CH)
            s = s + jnp.sum(v, axis=0)
            q = q + jnp.sum(v * v, axis=0)
        return s, q

    lane = lax.broadcasted_iota(jnp.int32, (1, CH), 1)
    even = lane % 2 == 0

    def packed(s, q):
        s = jnp.sum(s, axis=0, keepdims=True)
        q = jnp.sum(q, axis=0, keepdims=True)
        return jnp.where(even, s + pltpu.roll(s, CH - 1, 1), q + pltpu.roll(q, 1, 1))

    loads[0].wait()
    s, q = stats_of(
        xbuf[2 + f, 1 + r].astype(jnp.float32) for f in range(2) for r in range(4)
    )
    me_plane = cx * NY + y
    me_line = cz * NC + cc
    me = clip * NY + y
    plane[me_plane] = packed(s, q)

    pl.semaphore_wait(barrier, n_signals)

    def sends(offs, buf, at, n):
        cps = []
        for o in offs:
            cp = pltpu.make_async_remote_copy(
                src_ref=buf.at[at], dst_ref=buf.at[at],
                send_sem=st_send.at[n], recv_sem=st_recv.at[n],
                device_id=device(o), device_id_type=MESH,
            )
            cp.start()
            cps.append(cp)
        return cps

    def halo_sends(buf, n):
        own = buf.at[pl.ds(2, 2), pl.ds(1, 4)]
        first = buf.at[pl.ds(2, 2), 1]
        last = buf.at[pl.ds(2, 2), 4]
        plan = [
            (own, buf.at[pl.ds(0, 2), pl.ds(1, 4)], (nxt, y)),
            (last, buf.at[pl.ds(0, 2), 0], (nxt, up)),
            (first, buf.at[pl.ds(0, 2), 5], (nxt, down)),
            (last, buf.at[pl.ds(2, 2), 0], (clip, up)),
            (first, buf.at[pl.ds(2, 2), 5], (clip, down)),
        ]
        cps = []
        for m, (src, dst, dev) in enumerate(plan):
            cp = pltpu.make_async_remote_copy(
                src_ref=src, dst_ref=dst, send_sem=halo_send.at[n, m],
                recv_sem=halo_recv.at[n, m], device_id=dev, device_id_type=MESH,
            )
            cp.start()
            cps.append(cp)
        return cps

    def arrived(buf, count, n):
        got = buf.at[pl.ds(0, count)]
        pltpu.make_async_copy(got, got, st_recv.at[n]).wait()

    sent = sends(PLANE, plane, me_plane, 0)
    halo_1 = halo_sends(xbuf, 0)

    for cp in loads[1:]:
        cp.wait()
    own_id = ids[clip]
    blocks = jnp.float32(0)
    for k in range(NX * NZ):
        for c in range(NC):
            m = jnp.where(ids[k * NC + c] == own_id, jnp.float32(1), jnp.float32(0))
            blocks = blocks + m
            m = jnp.full((1, CH), m, jnp.float32)
            mask[k * NC + c] = m
            line_mask[(k % NZ) * NC + c, k // NZ : k // NZ + 1, :] = m
    prior_id = ids[jnp.maximum(clip - 1, 0)]
    same = jnp.where(prior_id == own_id, jnp.float32(1), jnp.float32(0))
    same = same * jnp.where(clip > 0, jnp.float32(1), jnp.float32(0))
    top = jnp.where(y > 0, jnp.float32(1), jnp.float32(0))
    bottom = jnp.where(y < NY - 1, jnp.float32(1), jnp.float32(0))
    one_count = 1.0 / (jnp.full((1, CH), blocks, jnp.float32) * (2 * 4 * NY * W * 4))
    zero = jnp.zeros((CH, CH), jnp.bfloat16)
    for cv in range(2):
        for dx in range(3):
            for dy in range(3):
                wts[cv, dx, dy, 0:CH, CH : 2 * CH] = zero
                wts[cv, dx, dy, 3 * CH : 4 * CH, 0:CH] = zero

    def finish(t, gain, shift):
        t = t + jnp.where(lane % 4 < 2, pltpu.roll(t, CH - 2, 1), pltpu.roll(t, 2, 1))
        t = t * one_count
        mean = jnp.where(even, t, pltpu.roll(t, 1, 1))
        square = jnp.where(even, pltpu.roll(t, CH - 1, 1), t)
        inverse = lax.rsqrt(square - mean * mean + EPS)
        scale = inverse * gain
        return 0.5 * scale, 0.5 * (shift - mean * scale)

    def tree(terms):
        while len(terms) > 1:
            terms = [sum(terms[k : k + 2][1:], terms[k]) for k in range(0, len(terms), 2)]
        return terms[0]

    def activate(buf, scale, offset):
        for r in range(6):
            row = top if r == 0 else bottom if r == 5 else None
            for j in range(4):
                keep = row
                if j < 2:
                    keep = same if row is None else same * row
                sc, of = (scale, offset) if keep is None else (scale * keep, offset * keep)
                h = buf[j, r].astype(jnp.float32) * sc + of
                v = h + h * jnp.tanh(h)
                act[r * W : (r + 1) * W, j * CH : (j + 1) * CH] = v.astype(jnp.bfloat16)

    def convolve(cv):
        lhs = jnp.concatenate([act[d * W : (d + 4) * W, :] for d in range(3)], axis=1)
        for dx in range(3):
            rhs = wts[cv, dx].reshape(3 * 4 * CH, 2 * CH)
            pbuf[dx] = jnp.dot(lhs, rhs, preferred_element_type=jnp.float32)

    col = lax.broadcasted_iota(jnp.int32, (W, CH), 0)

    def joined(f, r, bias):
        at = (slice(r * W, (r + 1) * W), slice(f * CH, (f + 1) * CH))
        left = jnp.where(col == 0, 0.0, pltpu.roll(pbuf[(0, *at)], 1, 0))
        right = jnp.where(col == W - 1, 0.0, pltpu.roll(pbuf[(2, *at)], W - 1, 0))
        return (left + pbuf[(1, *at)]) + (right + bias)

    arrived(plane, len(PLANE), 0)
    for k in range(NX):
        line[me_line, k : k + 1, :] = tree([plane[k * NY + n] for n in range(NY)])
    sent += sends(LINE, line, me_line, 1)
    for cp in w_loads:
        cp.wait()
    for cp in halo_1:
        cp.wait_recv()
    arrived(line, len(LINE), 1)
    t = tree([line[k] * line_mask[k] for k in range(NZ * NC)])
    t = tree([t[k : k + 1] for k in range(NX)])
    scale, offset = finish(t, vecs[0], vecs[1])
    activate(xbuf, scale, offset)
    convolve(0)

    def hidden_rows():
        for f in range(2):
            for r in range(4):
                v = joined(f, r, vecs[2]).astype(jnp.bfloat16)
                hbuf[2 + f, 1 + r] = v
                yield v.astype(jnp.float32)

    s, q = stats_of(hidden_rows())
    every[me] = packed(s, q)
    sent += sends(EVERY, every, me, 2)
    halo_2 = halo_sends(hbuf, 1)
    for cp in halo_2:
        cp.wait_recv()
    arrived(every, len(EVERY), 2)
    t = tree(
        [
            tree([every[k * NY + n] for n in range(NY)]) * mask[k]
            for k in range(NX * NZ * NC)
        ]
    )
    scale, offset = finish(t, vecs[3], vecs[4])
    activate(hbuf, scale, offset)
    convolve(1)
    for f in range(2):
        for r in range(4):
            v = joined(f, r, vecs[5]) + xbuf[2 + f, 1 + r].astype(jnp.float32)
            out_ref[f, r] = v.astype(jnp.bfloat16)
    for cp in sent + halo_1 + halo_2:
        cp.wait_send()


def per_device(x, ids, g1, s1, k1, b1, g2, s2, k2, b2):
    vec = [v.reshape(1, CH) for v in (g1, s1, b1, g2, s2, b2)]
    g1, s1, b1, g2, s2, b2 = vec
    anywhere = pl.BlockSpec(memory_space=pl.ANY)
    operands = [
        pltpu.with_memory_space_constraint(v, pltpu.HBM)
        for v in (x, ids, g1, s1, k1, b1, g2, s2, k2, b2)
    ]
    bf16, f32 = jnp.bfloat16, jnp.float32
    return pl.pallas_call(
        kernel,
        out_shape=jax.ShapeDtypeStruct(x.shape, bf16),
        in_specs=[anywhere] * 10,
        out_specs=pl.BlockSpec(memory_space=pltpu.VMEM),
        scratch_shapes=[
            pltpu.VMEM((4, 6, W, CH), bf16),
            pltpu.VMEM((4, 6, W, CH), bf16),
            pltpu.VMEM((6 * W, 4 * CH), bf16),
            pltpu.VMEM((2, 3, 3, 4 * CH, 2 * CH), bf16),
            pltpu.VMEM((3, 4 * W, 2 * CH), f32),
            pltpu.SMEM((64,), jnp.int32),
            pltpu.VMEM((6, 1, CH), f32),
            pltpu.VMEM((NX * NY, 1, CH), f32),
            pltpu.VMEM((NZ * NC, NX, CH), f32),
            pltpu.VMEM((NX * NZ * NC * NY, 1, CH), f32),
            pltpu.VMEM((NZ * NC, NX, CH), f32),
            pltpu.VMEM((NX * NZ * NC, 1, CH), f32),
            pltpu.SemaphoreType.DMA((8,)),
            pltpu.SemaphoreType.DMA((2, 18)),
            pltpu.SemaphoreType.DMA((2, 5)),
            pltpu.SemaphoreType.DMA((2, 5)),
            pltpu.SemaphoreType.DMA((3,)),
            pltpu.SemaphoreType.DMA((3,)),
        ],
        compiler_params=pltpu.CompilerParams(
            collective_id=0, has_side_effects=True, vmem_limit_bytes=48 * 1024 * 1024
        ),
        cost_estimate=pl.CostEstimate(
            flops=4 * 1024 * 27 * CH * CH, bytes_accessed=2500000, transcendentals=800000
        ),
    )(*operands)


def solution(mesh):
    placed = (P("clip", "slab", None, None), P(), P(), P(), P(), P(), P(), P(), P(), P())
    return jax.shard_map(
        per_device,
        mesh=mesh,
        in_specs=placed,
        out_specs=P("clip", "slab", None, None),
        check_vma=False,
    )
```

```python
import functools

import jax
import jax.numpy as jnp
from jax import lax
from jax.experimental import pallas as pl
from jax.experimental.pallas import tpu as pltpu
from jax.sharding import PartitionSpec as P

MESH = pl.DeviceIdType.MESH
NX, NZ, NC, NY = 4, 8, 2, 4
CH = 128
W = 128
EPS = 1e-06


def hops(dx, dz, dy):
    return min(dx, NX - dx) + min(dz, NZ - dz) + min(dy, NY - dy)


def offsets(nx, ny, nz, nc):
    every = [
        (dx, dy, dz, dc)
        for dx in range(nx) for dy in range(ny) for dz in range(nz) for dc in range(nc)
    ]
    return sorted(every[1:], key=lambda o: -hops(o[0], o[2], o[1]))


NEAR = offsets(NX, 1, 1, NC)
FAR = offsets(1, NY, NZ, 1)
EVERY = offsets(NX, NY, NZ, NC)
SIDE = [[o for o in EVERY if o[0] == dx] for dx in range(NX)]
BEYOND = sorted({o[2:] for o in SIDE[2]}, key=lambda o: -hops(2, o[0], 0))


def kernel(
    x_hbm, ids_hbm, g1, s1, k1, b1, g2, s2, k2, b2, out_ref,
    xbuf, hbuf, act, wts, pbuf, ids, vecs, near, parts, far, every, far_mask, mask,
    load_sem, w_sem, halo_send, halo_recv, st_send, st_recv, near_in, far_in,
):
    clip = lax.axis_index("clip")
    y = lax.axis_index("slab")
    cx = clip // (NZ * NC)
    cz = (clip // NC) % NZ
    cc = clip % NC
    clips = NX * NZ * NC

    def device(o):
        dx, dy, dz, dc = o
        at = (cx + dx) % NX if dx else cx
        at = at * NZ + ((cz + dz) % NZ if dz else cz)
        at = at * NC + ((cc + dc) % NC if dc else cc)
        return (at, (y + dy) % NY if dy else y)

    nxt, prv = (clip + 1) % clips, (clip + clips - 1) % clips
    up, down = (y + 1) % NY, (y + NY - 1) % NY

    barrier = pltpu.get_barrier_semaphore()

    def greet(dev):
        pl.semaphore_signal(barrier, inc=1, device_id=dev, device_id_type=MESH)

    def at(dx, dy, dz, core):
        chip = ((cx + dx) % NX) * NZ + (cz + dz) % NZ
        return (chip * NC + core, (y + dy) % NY)

    for dx in range(1, NX):
        greet(at(dx, 0, 0, 0))
    for side in (up, down):
        greet((clip - cc, side))

    @pl.when(cc == 0)
    def _():
        for side in (y, up, down):
            greet(((clip + clips - NC) % clips, side))
        greet((clip + 1, y))

    @pl.when(cc == 1)
    def _():
        greet((clip - 1, y))

    for _, dy, dz, _ in FAR:
        greet(at(0, dy, dz, 1))
    heard_near = 2 * (NX - 1) + 1 + 4 + 3
    heard_far = 2 * len(FAR) + 1

    loads = [pltpu.make_async_copy(x_hbm, xbuf.at[pl.ds(2, 2), pl.ds(1, 4)], load_sem.at[0])]
    loads.append(pltpu.make_async_copy(ids_hbm, ids, load_sem.at[1]))
    for n, v in enumerate((g1, s1, b1, g2, s2, b2)):
        loads.append(pltpu.make_async_copy(v, vecs.at[n], load_sem.at[2 + n]))
    for cp in loads:
        cp.start()
    w_loads = []
    for cv, k in enumerate((k1, k2)):
        for dt in range(3):
            for dx in range(3):
                for i in range(2):
                    j = dt + i
                    cp = pltpu.make_async_copy(
                        k.at[dt, :, dx],
                        wts.at[cv, dx, :, pl.ds(j * CH, CH), pl.ds(i * CH, CH)],
                        w_sem.at[cv, len(w_loads) % 18],
                    )
                    cp.start()
                    w_loads.append(cp)

    def stats_of(rows):
        s = jnp.zeros((8, CH), jnp.float32)
        q = jnp.zeros((8, CH), jnp.float32)
        for v in rows:
            v = v.reshape(W // 8, 8, CH)
            s = s + jnp.sum(v, axis=0)
            q = q + jnp.sum(v * v, axis=0)
        return s, q

    lane = lax.broadcasted_iota(jnp.int32, (1, CH), 1)
    even = lane % 2 == 0

    def packed(s, q):
        s = jnp.sum(s, axis=0, keepdims=True)
        q = jnp.sum(q, axis=0, keepdims=True)
        return jnp.where(even, s + pltpu.roll(s, CH - 1, 1), q + pltpu.roll(q, 1, 1))

    every[...] = jnp.zeros_like(every)
    loads[0].wait()
    s, q = stats_of(
        xbuf[2 + f, 1 + r].astype(jnp.float32) for f in range(2) for r in range(4)
    )
    me_near = cx * NC + cc
    me_far = y * NZ + cz
    me = clip * NY + y
    near[me_near] = packed(s, q)

    @pl.when(cc == 0)
    def _():
        pl.semaphore_wait(barrier, heard_near)
        pl.semaphore_signal(near_in, inc=1, device_id=(clip + 1, y), device_id_type=MESH)

    @pl.when(cc == 1)
    def _():
        pl.semaphore_wait(near_in, 1)

    def sends(offs, buf, at, n):
        return copies([(o, buf.at[at], buf.at[at]) for o in offs], n)

    def copies(plan, n):
        cps = []
        for o, src, dst in plan:
            cp = pltpu.make_async_remote_copy(
                src_ref=src, dst_ref=dst,
                send_sem=st_send.at[n], recv_sem=st_recv.at[n],
                device_id=device(o), device_id_type=MESH,
            )
            cp.start()
            cps.append(cp)
        return cps

    def halo_sends(plan, n):
        cps = []
        for m, (src, dst, dev) in plan:
            cp = pltpu.make_async_remote_copy(
                src_ref=src, dst_ref=dst, send_sem=halo_send.at[n, m],
                recv_sem=halo_recv.at[n, m], device_id=dev, device_id_type=MESH,
            )
            cp.start()
            cps.append(cp)
        return cps

    frames = pl.ds(2, 2)
    carried = pl.ds(0, 2)

    def input_halo():
        own, top_row, low_row = xbuf.at[frames, pl.ds(1, 4)], xbuf.at[frames, 1], xbuf.at[frames, 4]
        plan = [
            (own, xbuf.at[carried, pl.ds(1, 4)], (nxt, y)),
            (low_row, xbuf.at[carried, 0], (nxt, up)),
            (top_row, xbuf.at[carried, 5], (nxt, down)),
            (low_row, xbuf.at[frames, 0], (clip, up)),
            (top_row, xbuf.at[frames, 5], (clip, down)),
        ]
        return halo_sends(enumerate(plan), 0)

    def hidden_halo(part):
        rows = pl.ds(1 + 2 * part, 2)
        edge, land, side = ((1, 5, down), (4, 0, up))[part]
        plan = [
            (hbuf.at[frames, rows], hbuf.at[carried, rows], (nxt, y)),
            (hbuf.at[frames, edge], hbuf.at[carried, land], (nxt, side)),
            (hbuf.at[frames, edge], hbuf.at[frames, land], (clip, side)),
        ]
        return halo_sends([(3 * part + m, copy) for m, copy in enumerate(plan)], 1)

    def done(buf, count, sem):
        got = buf.at[pl.ds(0, count)]
        pltpu.make_async_copy(got, got, sem).wait()

    def arrived(buf, count, n):
        done(buf, count, st_recv.at[n])

    def reached(dz, dc):
        here = cz * NC + cc
        there = ((cz + dz) % NZ) * NC + (cc + dc) % NC
        return jnp.where(cx < 2, here - there, there - here) > 0

    sent = sends(NEAR, near, me_near, 0)
    halo_1 = input_halo()

    for cp in loads[1:]:
        cp.wait()
    own_id = ids[clip]
    blocks = jnp.float32(0)
    for k in range(NX * NZ):
        for c in range(NC):
            m = jnp.where(ids[k * NC + c] == own_id, jnp.float32(1), jnp.float32(0))
            blocks = blocks + m
            m = jnp.full((1, CH), m, jnp.float32)
            mask[k * NC + c] = m
    column = [ids[(dx * NZ + cz) * NC + c] for dx in range(NX) for c in range(NC)]
    for k in range(NZ):
        target = ids[(cx * NZ + k) * NC + cc]
        for n, member in enumerate(column):
            m = jnp.where(member == target, jnp.float32(1), jnp.float32(0))
            far_mask[k * NX * NC + n] = jnp.full((1, CH), m, jnp.float32)
    prior_id = ids[jnp.maximum(clip - 1, 0)]
    same = jnp.where(prior_id == own_id, jnp.float32(1), jnp.float32(0))
    same = same * jnp.where(clip > 0, jnp.float32(1), jnp.float32(0))
    top = jnp.where(y > 0, jnp.float32(1), jnp.float32(0))
    bottom = jnp.where(y < NY - 1, jnp.float32(1), jnp.float32(0))
    one_count = 1.0 / (jnp.full((1, CH), blocks, jnp.float32) * (2 * 4 * NY * W * 4))
    zero = jnp.zeros((CH, CH), jnp.bfloat16)
    for cv in range(2):
        for dx in range(3):
            for dy in range(3):
                wts[cv, dx, dy, 0:CH, CH : 2 * CH] = zero
                wts[cv, dx, dy, 3 * CH : 4 * CH, 0:CH] = zero

    def finish(t, gain, shift):
        t = t + jnp.where(lane % 4 < 2, pltpu.roll(t, CH - 2, 1), pltpu.roll(t, 2, 1))
        t = t * one_count
        mean = jnp.where(even, t, pltpu.roll(t, 1, 1))
        square = jnp.where(even, pltpu.roll(t, CH - 1, 1), t)
        inverse = lax.rsqrt(square - mean * mean + EPS)
        scale = inverse * gain
        return 0.5 * scale, 0.5 * (shift - mean * scale)

    def tree(terms):
        while len(terms) > 1:
            terms = [sum(terms[k : k + 2][1:], terms[k]) for k in range(0, len(terms), 2)]
        return terms[0]

    def activate(buf, scale, offset, frames):
        for r in range(6):
            row = top if r == 0 else bottom if r == 5 else None
            for j in frames:
                keep = row
                if j < 2:
                    keep = same if row is None else same * row
                sc, of = (scale, offset) if keep is None else (scale * keep, offset * keep)
                h = buf[j, r].astype(jnp.float32) * sc + of
                v = h + h * jnp.tanh(h)
                act[r * W : (r + 1) * W, j * CH : (j + 1) * CH] = v.astype(jnp.bfloat16)

    def convolve(cv, row, rows, frames, more=False):
        out = slice(row * W, (row + rows) * W)
        k = slice(frames[0] * CH, (frames[-1] + 1) * CH)
        lhs = jnp.concatenate(
            [act[(row + d) * W : (row + d + rows) * W, k] for d in range(3)], axis=1
        )
        for dx in range(3):
            rhs = jnp.concatenate([wts[cv, dx, d, k, :] for d in range(3)], axis=0)
            p = jnp.dot(lhs, rhs, preferred_element_type=jnp.float32)
            pbuf[dx, out] = pbuf[dx, out] + p if more else p

    col = lax.broadcasted_iota(jnp.int32, (W, CH), 0)

    def joined(f, r, bias):
        at = (slice(r * W, (r + 1) * W), slice(f * CH, (f + 1) * CH))
        left = jnp.where(col == 0, 0.0, pltpu.roll(pbuf[(0, *at)], 1, 0))
        right = jnp.where(col == W - 1, 0.0, pltpu.roll(pbuf[(2, *at)], W - 1, 0))
        return (left + pbuf[(1, *at)]) + (right + bias)

    @pl.when(cc == 1)
    def _():
        pl.semaphore_wait(barrier, heard_far)
        pl.semaphore_signal(far_in, inc=1, device_id=(clip - 1, y), device_id_type=MESH)

    @pl.when(cc == 0)
    def _():
        pl.semaphore_wait(far_in, 1)

    arrived(near, len(NEAR), 0)
    for k in range(NZ):
        parts[k] = tree([near[n] * far_mask[k * NX * NC + n] for n in range(NX * NC)])
    far[me_far] = parts[cz]
    sent += copies([(o, parts.at[(cz + o[2]) % NZ], far.at[me_far]) for o in FAR], 1)
    for cp in w_loads:
        cp.wait()
    for cp in halo_1:
        cp.wait_recv()
    arrived(far, len(FAR), 1)
    t = tree([far[k] for k in range(NY * NZ)])
    scale, offset = finish(t, vecs[0], vecs[1])
    activate(xbuf, scale, offset, range(4))

    def hidden_rows(part):
        for f in range(2):
            for r in range(2 * part, 2 * part + 2):
                v = joined(f, r, vecs[2]).astype(jnp.bfloat16)
                hbuf[2 + f, 1 + r] = v
                yield v.astype(jnp.float32)

    convolve(0, 0, 2, range(4))
    s, q = stats_of(hidden_rows(0))
    convolve(0, 2, 2, range(4))
    s2, q2 = stats_of(hidden_rows(1))
    s, q = s + s2, q + q2
    every[me] = packed(s, q)
    for dz, dc in BEYOND:

        @pl.when(reached(dz, dc))
        def _():
            sends([o for o in SIDE[2] if o[2:] == (dz, dc)], every, me, 5 + dz * NC + dc)

    @pl.when(cx < NX - 1)
    def _():
        sends(SIDE[1], every, me, 3)

    @pl.when(cx > 0)
    def _():
        sends(SIDE[3], every, me, 4)

    sent += sends(SIDE[0], every, me, 2)
    halo_2 = hidden_halo(0) + hidden_halo(1)
    arrived(every, len(SIDE[0]), 2)

    @pl.when(cx > 0)
    def _():
        arrived(every, len(SIDE[1]), 3)

    @pl.when(cx < NX - 1)
    def _():
        arrived(every, len(SIDE[3]), 4)

    for dz, dc in BEYOND:

        @pl.when(reached(-dz, dc))
        def _():
            arrived(every, NY, 5 + dz * NC + dc)

    t = tree(
        [
            tree([every[k * NY + n] for n in range(NY)]) * mask[k]
            for k in range(NX * NZ * NC)
        ]
    )
    scale, offset = finish(t, vecs[3], vecs[4])
    for m in (2, 5):
        halo_2[m].wait_recv()
    activate(hbuf, scale, offset, range(2, 4))
    convolve(1, 0, 4, range(2, 4))
    for m in (0, 1, 3, 4):
        halo_2[m].wait_recv()
    activate(hbuf, scale, offset, range(2))
    convolve(1, 0, 4, range(2), more=True)
    for f in range(2):
        for r in range(4):
            v = joined(f, r, vecs[5]) + xbuf[2 + f, 1 + r].astype(jnp.float32)
            out_ref[f, r] = v.astype(jnp.bfloat16)
    for cp in sent + halo_1 + halo_2:
        cp.wait_send()

    @pl.when(cx < NX - 1)
    def _():
        done(every, len(SIDE[1]), st_send.at[3])

    @pl.when(cx > 0)
    def _():
        done(every, len(SIDE[3]), st_send.at[4])

    for dz, dc in BEYOND:

        @pl.when(reached(dz, dc))
        def _():
            done(every, NY, st_send.at[5 + dz * NC + dc])


def per_device(x, ids, g1, s1, k1, b1, g2, s2, k2, b2):
    vec = [v.reshape(1, CH) for v in (g1, s1, b1, g2, s2, b2)]
    g1, s1, b1, g2, s2, b2 = vec
    anywhere = pl.BlockSpec(memory_space=pl.ANY)
    operands = [
        pltpu.with_memory_space_constraint(v, pltpu.HBM)
        for v in (x, ids, g1, s1, k1, b1, g2, s2, k2, b2)
    ]
    bf16, f32 = jnp.bfloat16, jnp.float32
    return pl.pallas_call(
        kernel,
        out_shape=jax.ShapeDtypeStruct(x.shape, bf16),
        in_specs=[anywhere] * 10,
        out_specs=pl.BlockSpec(memory_space=pltpu.VMEM),
        scratch_shapes=[
            pltpu.VMEM((4, 6, W, CH), bf16),
            pltpu.VMEM((4, 6, W, CH), bf16),
            pltpu.VMEM((6 * W, 4 * CH), bf16),
            pltpu.VMEM((2, 3, 3, 4 * CH, 2 * CH), bf16),
            pltpu.VMEM((3, 4 * W, 2 * CH), f32),
            pltpu.SMEM((64,), jnp.int32),
            pltpu.VMEM((6, 1, CH), f32),
            pltpu.VMEM((NX * NC, 1, CH), f32),
            pltpu.VMEM((NZ, 1, CH), f32),
            pltpu.VMEM((NY * NZ, 1, CH), f32),
            pltpu.VMEM((NX * NZ * NC * NY, 1, CH), f32),
            pltpu.VMEM((NZ * NX * NC, 1, CH), f32),
            pltpu.VMEM((NX * NZ * NC, 1, CH), f32),
            pltpu.SemaphoreType.DMA((8,)),
            pltpu.SemaphoreType.DMA((2, 18)),
            pltpu.SemaphoreType.DMA((2, 7)),
            pltpu.SemaphoreType.DMA((2, 7)),
            pltpu.SemaphoreType.DMA((5 + NZ * NC,)),
            pltpu.SemaphoreType.DMA((5 + NZ * NC,)),
            pltpu.SemaphoreType.REGULAR,
            pltpu.SemaphoreType.REGULAR,
        ],
        compiler_params=pltpu.CompilerParams(
            collective_id=0, has_side_effects=True, vmem_limit_bytes=48 * 1024 * 1024
        ),
        cost_estimate=pl.CostEstimate(
            flops=4 * 1024 * 27 * CH * CH, bytes_accessed=2500000, transcendentals=800000
        ),
    )(*operands)


def solution(mesh):
    placed = (P("clip", "slab", None, None), P(), P(), P(), P(), P(), P(), P(), P(), P())
    return jax.shard_map(
        per_device,
        mesh=mesh,
        in_specs=placed,
        out_specs=P("clip", "slab", None, None),
        check_vma=False,
    )
```

```python
import functools

import jax
import jax.numpy as jnp
from jax import lax
from jax.experimental import pallas as pl
from jax.experimental.pallas import tpu as pltpu
from jax.sharding import PartitionSpec as P

MESH = pl.DeviceIdType.MESH
NX, NZ, NC, NY = 4, 8, 2, 4
CH = 128
W = 128
EPS = 1e-06


def hops(dx, dz, dy):
    return min(dx, NX - dx) + min(dz, NZ - dz) + min(dy, NY - dy)


def offsets(nx, ny, nz, nc):
    every = [
        (dx, dy, dz, dc)
        for dx in range(nx) for dy in range(ny) for dz in range(nz) for dc in range(nc)
    ]
    return sorted(every[1:], key=lambda o: -hops(o[0], o[2], o[1]))


NEAR = offsets(NX, 1, 1, NC)
FAR = offsets(1, NY, NZ, 1)
EVERY = offsets(NX, NY, NZ, NC)
SIDE = [[o for o in EVERY if o[0] == dx] for dx in range(NX)]
BEYOND = sorted({o[2:] for o in SIDE[2]}, key=lambda o: -hops(2, o[0], 0))


def kernel(
    x_hbm, ids_hbm, g1, s1, k1, b1, g2, s2, k2, b2, out_ref,
    xbuf, hbuf, act, wts, pbuf, ids, vecs, near, parts, far, every, far_mask, mask,
    load_sem, w_sem, halo_send, halo_recv, st_send, st_recv, near_in, far_in,
):
    clip = lax.axis_index("clip")
    y = lax.axis_index("slab")
    cx = clip // (NZ * NC)
    cz = (clip // NC) % NZ
    cc = clip % NC
    clips = NX * NZ * NC

    def device(o):
        dx, dy, dz, dc = o
        at = (cx + dx) % NX if dx else cx
        at = at * NZ + ((cz + dz) % NZ if dz else cz)
        at = at * NC + ((cc + dc) % NC if dc else cc)
        return (at, (y + dy) % NY if dy else y)

    nxt, prv = (clip + 1) % clips, (clip + clips - 1) % clips
    up, down = (y + 1) % NY, (y + NY - 1) % NY

    barrier = pltpu.get_barrier_semaphore()

    def greet(dev):
        pl.semaphore_signal(barrier, inc=1, device_id=dev, device_id_type=MESH)

    def at(dx, dy, dz, core):
        chip = ((cx + dx) % NX) * NZ + (cz + dz) % NZ
        return (chip * NC + core, (y + dy) % NY)

    for dx in range(1, NX):
        greet(at(dx, 0, 0, 0))
    for side in (up, down):
        greet((clip - cc, side))

    @pl.when(cc == 0)
    def _():
        for side in (y, up, down):
            greet(((clip + clips - NC) % clips, side))
        greet((clip + 1, y))

    @pl.when(cc == 1)
    def _():
        greet((clip - 1, y))

    for _, dy, dz, _ in FAR:
        greet(at(0, dy, dz, 1))
    heard_near = 2 * (NX - 1) + 1 + 4 + 3
    heard_far = 2 * len(FAR) + 1

    loads = [pltpu.make_async_copy(x_hbm, xbuf.at[pl.ds(2, 2), pl.ds(1, 4)], load_sem.at[0])]
    loads.append(pltpu.make_async_copy(ids_hbm, ids, load_sem.at[1]))
    for n, v in enumerate((g1, s1, b1, g2, s2, b2)):
        loads.append(pltpu.make_async_copy(v, vecs.at[n], load_sem.at[2 + n]))
    for cp in loads:
        cp.start()
    w_loads = []
    for cv, k in enumerate((k1, k2)):
        for dt in range(3):
            for dx in range(3):
                for i in range(2):
                    j = dt + i
                    cp = pltpu.make_async_copy(
                        k.at[dt, :, dx],
                        wts.at[cv, dx, :, pl.ds(j * CH, CH), pl.ds(i * CH, CH)],
                        w_sem.at[cv, len(w_loads) % 18],
                    )
                    cp.start()
                    w_loads.append(cp)

    def stats_of(rows):
        s = jnp.zeros((8, CH), jnp.float32)
        q = jnp.zeros((8, CH), jnp.float32)
        for v in rows:
            v = v.reshape(W // 8, 8, CH)
            s = s + jnp.sum(v, axis=0)
            q = q + jnp.sum(v * v, axis=0)
        return s, q

    lane = lax.broadcasted_iota(jnp.int32, (1, CH), 1)
    even = lane % 2 == 0

    def packed(s, q):
        s = jnp.sum(s, axis=0, keepdims=True)
        q = jnp.sum(q, axis=0, keepdims=True)
        return jnp.where(even, s + pltpu.roll(s, CH - 1, 1), q + pltpu.roll(q, 1, 1))

    every[...] = jnp.zeros_like(every)
    loads[0].wait()
    s, q = stats_of(
        xbuf[2 + f, 1 + r].astype(jnp.float32) for f in range(2) for r in range(4)
    )
    me_near = cx * NC + cc
    me_far = y * NZ + cz
    me = clip * NY + y
    near[me_near] = packed(s, q)

    @pl.when(cc == 0)
    def _():
        pl.semaphore_wait(barrier, heard_near)
        pl.semaphore_signal(near_in, inc=1, device_id=(clip + 1, y), device_id_type=MESH)

    @pl.when(cc == 1)
    def _():
        pl.semaphore_wait(near_in, 1)

    def sends(offs, buf, at, n):
        return copies([(o, buf.at[at], buf.at[at]) for o in offs], n)

    def copies(plan, n):
        cps = []
        for o, src, dst in plan:
            cp = pltpu.make_async_remote_copy(
                src_ref=src, dst_ref=dst,
                send_sem=st_send.at[n], recv_sem=st_recv.at[n],
                device_id=device(o), device_id_type=MESH,
            )
            cp.start()
            cps.append(cp)
        return cps

    def halo(plan, n):
        return [
            pltpu.make_async_remote_copy(
                src_ref=src, dst_ref=dst, send_sem=halo_send.at[n, m],
                recv_sem=halo_recv.at[n, m], device_id=dev, device_id_type=MESH,
            )
            for m, (src, dst, dev) in plan
        ]

    def start(cps):
        for cp in cps:
            cp.start()

    frames = pl.ds(2, 2)
    carried = pl.ds(0, 2)

    def input_halo():
        own, top_row, low_row = xbuf.at[frames, pl.ds(1, 4)], xbuf.at[frames, 1], xbuf.at[frames, 4]
        plan = [
            (own, xbuf.at[carried, pl.ds(1, 4)], (nxt, y)),
            (low_row, xbuf.at[carried, 0], (nxt, up)),
            (top_row, xbuf.at[carried, 5], (nxt, down)),
            (low_row, xbuf.at[frames, 0], (clip, up)),
            (top_row, xbuf.at[frames, 5], (clip, down)),
        ]
        return halo(enumerate(plan), 0)

    def hidden_halo(part):
        rows = pl.ds(1 + 2 * part, 2)
        edge, land, side = ((1, 5, down), (4, 0, up))[part]
        plan = [
            (hbuf.at[frames, rows], hbuf.at[carried, rows], (nxt, y)),
            (hbuf.at[frames, edge], hbuf.at[carried, land], (nxt, side)),
            (hbuf.at[frames, edge], hbuf.at[frames, land], (clip, side)),
        ]
        return halo([(3 * part + m, copy) for m, copy in enumerate(plan)], 1)

    def done(buf, count, sem):
        got = buf.at[pl.ds(0, count)]
        pltpu.make_async_copy(got, got, sem).wait()

    def arrived(buf, count, n):
        done(buf, count, st_recv.at[n])

    def reached(dz, dc):
        here = cz * NC + cc
        there = ((cz + dz) % NZ) * NC + (cc + dc) % NC
        return jnp.where(cx < 2, here - there, there - here) > 0

    sent = sends(NEAR, near, me_near, 0)
    halo_1 = input_halo()
    start(halo_1)

    for cp in loads[1:]:
        cp.wait()
    own_id = ids[clip]
    blocks = jnp.float32(0)
    for k in range(NX * NZ):
        for c in range(NC):
            m = jnp.where(ids[k * NC + c] == own_id, jnp.float32(1), jnp.float32(0))
            blocks = blocks + m
            m = jnp.full((1, CH), m, jnp.float32)
            mask[k * NC + c] = m
    column = [ids[(dx * NZ + cz) * NC + c] for dx in range(NX) for c in range(NC)]
    for k in range(NZ):
        target = ids[(cx * NZ + k) * NC + cc]
        for n, member in enumerate(column):
            m = jnp.where(member == target, jnp.float32(1), jnp.float32(0))
            far_mask[k * NX * NC + n] = jnp.full((1, CH), m, jnp.float32)
    prior_id = ids[jnp.maximum(clip - 1, 0)]
    same = jnp.where(prior_id == own_id, jnp.float32(1), jnp.float32(0))
    same = same * jnp.where(clip > 0, jnp.float32(1), jnp.float32(0))
    top = jnp.where(y > 0, jnp.float32(1), jnp.float32(0))
    bottom = jnp.where(y < NY - 1, jnp.float32(1), jnp.float32(0))
    one_count = 1.0 / (jnp.full((1, CH), blocks, jnp.float32) * (2 * 4 * NY * W * 4))
    zero = jnp.zeros((CH, CH), jnp.bfloat16)
    for cv in range(2):
        for dx in range(3):
            for dy in range(3):
                wts[cv, dx, dy, 0:CH, CH : 2 * CH] = zero
                wts[cv, dx, dy, 3 * CH : 4 * CH, 0:CH] = zero

    def finish(t, gain, shift):
        t = t + jnp.where(lane % 4 < 2, pltpu.roll(t, CH - 2, 1), pltpu.roll(t, 2, 1))
        t = t * one_count
        mean = jnp.where(even, t, pltpu.roll(t, 1, 1))
        square = jnp.where(even, pltpu.roll(t, CH - 1, 1), t)
        inverse = lax.rsqrt(square - mean * mean + EPS)
        scale = inverse * gain
        return 0.5 * scale, 0.5 * (shift - mean * scale)

    def tree(terms):
        while len(terms) > 1:
            terms = [sum(terms[k : k + 2][1:], terms[k]) for k in range(0, len(terms), 2)]
        return terms[0]

    def activate(buf, scale, offset, frames):
        for r in range(6):
            row = top if r == 0 else bottom if r == 5 else None
            for j in frames:
                keep = row
                if j < 2:
                    keep = same if row is None else same * row
                sc, of = (scale, offset) if keep is None else (scale * keep, offset * keep)
                h = buf[j, r].astype(jnp.float32) * sc + of
                v = h + h * jnp.tanh(h)
                act[r * W : (r + 1) * W, j * CH : (j + 1) * CH] = v.astype(jnp.bfloat16)

    def convolve(cv, row, rows, frames, more=False):
        out = slice(row * W, (row + rows) * W)
        k = slice(frames[0] * CH, (frames[-1] + 1) * CH)
        lhs = jnp.concatenate(
            [act[(row + d) * W : (row + d + rows) * W, k] for d in range(3)], axis=1
        )
        for dx in range(3):
            rhs = jnp.concatenate([wts[cv, dx, d, k, :] for d in range(3)], axis=0)
            p = jnp.dot(lhs, rhs, preferred_element_type=jnp.float32)
            pbuf[dx, out] = pbuf[dx, out] + p if more else p

    col = lax.broadcasted_iota(jnp.int32, (W, CH), 0)

    def joined(f, r, bias):
        at = (slice(r * W, (r + 1) * W), slice(f * CH, (f + 1) * CH))
        left = jnp.where(col == 0, 0.0, pltpu.roll(pbuf[(0, *at)], 1, 0))
        right = jnp.where(col == W - 1, 0.0, pltpu.roll(pbuf[(2, *at)], W - 1, 0))
        return (left + pbuf[(1, *at)]) + (right + bias)

    @pl.when(cc == 1)
    def _():
        pl.semaphore_wait(barrier, heard_far)
        pl.semaphore_signal(far_in, inc=1, device_id=(clip - 1, y), device_id_type=MESH)

    @pl.when(cc == 0)
    def _():
        pl.semaphore_wait(far_in, 1)

    arrived(near, len(NEAR), 0)
    for k in range(NZ):
        parts[k] = tree([near[n] * far_mask[k * NX * NC + n] for n in range(NX * NC)])
    far[me_far] = parts[cz]
    sent += copies([(o, parts.at[(cz + o[2]) % NZ], far.at[me_far]) for o in FAR], 1)
    for cp in w_loads:
        cp.wait()
    for cp in halo_1:
        cp.wait_recv()
    arrived(far, len(FAR), 1)
    t = tree([far[k] for k in range(NY * NZ)])
    scale, offset = finish(t, vecs[0], vecs[1])
    activate(xbuf, scale, offset, range(4))

    def hidden_rows(part):
        for f in range(2):
            for r in range(2 * part, 2 * part + 2):
                v = joined(f, r, vecs[2]).astype(jnp.bfloat16)
                hbuf[2 + f, 1 + r] = v
                yield v.astype(jnp.float32)

    convolve(0, 0, 2, range(4))
    s, q = stats_of(hidden_rows(0))
    ahead = jnp.logical_and(cz == NZ - 1, cc == 1)
    halo_2 = hidden_halo(0) + hidden_halo(1)

    @pl.when(ahead)
    def _():
        start(halo_2[:1])

    convolve(0, 2, 2, range(4))
    s2, q2 = stats_of(hidden_rows(1))
    s, q = s + s2, q + q2
    every[me] = packed(s, q)
    @pl.when(cx > 0)
    def _():
        sends(SIDE[3], every, me, 4)

    for dz, dc in BEYOND:

        @pl.when(reached(dz, dc))
        def _():
            sends([o for o in SIDE[2] if o[2:] == (dz, dc)], every, me, 5 + dz * NC + dc)

    sent += sends(SIDE[0], every, me, 2)
    @pl.when(cx < NX - 1)
    def _():
        sends(SIDE[1], every, me, 3)


    @pl.when(jnp.logical_not(ahead))
    def _():
        start(halo_2[:1])

    start(halo_2[1:])
    arrived(every, len(SIDE[0]), 2)

    @pl.when(cx > 0)
    def _():
        arrived(every, len(SIDE[1]), 3)

    @pl.when(cx < NX - 1)
    def _():
        arrived(every, len(SIDE[3]), 4)

    for dz, dc in BEYOND:

        @pl.when(reached(-dz, dc))
        def _():
            arrived(every, NY, 5 + dz * NC + dc)

    t = tree(
        [
            tree([every[k * NY + n] for n in range(NY)]) * mask[k]
            for k in range(NX * NZ * NC)
        ]
    )
    scale, offset = finish(t, vecs[3], vecs[4])
    for m in (2, 5):
        halo_2[m].wait_recv()
    activate(hbuf, scale, offset, range(2, 4))
    convolve(1, 0, 4, range(2, 4))
    for m in (0, 1, 3, 4):
        halo_2[m].wait_recv()
    activate(hbuf, scale, offset, range(2))
    convolve(1, 0, 4, range(2), more=True)
    for f in range(2):
        for r in range(4):
            v = joined(f, r, vecs[5]) + xbuf[2 + f, 1 + r].astype(jnp.float32)
            out_ref[f, r] = v.astype(jnp.bfloat16)
    for cp in sent + halo_1 + halo_2:
        cp.wait_send()

    @pl.when(cx < NX - 1)
    def _():
        done(every, len(SIDE[1]), st_send.at[3])

    @pl.when(cx > 0)
    def _():
        done(every, len(SIDE[3]), st_send.at[4])

    for dz, dc in BEYOND:

        @pl.when(reached(dz, dc))
        def _():
            done(every, NY, st_send.at[5 + dz * NC + dc])


def per_device(x, ids, g1, s1, k1, b1, g2, s2, k2, b2):
    vec = [v.reshape(1, CH) for v in (g1, s1, b1, g2, s2, b2)]
    g1, s1, b1, g2, s2, b2 = vec
    anywhere = pl.BlockSpec(memory_space=pl.ANY)
    operands = [
        pltpu.with_memory_space_constraint(v, pltpu.HBM)
        for v in (x, ids, g1, s1, k1, b1, g2, s2, k2, b2)
    ]
    bf16, f32 = jnp.bfloat16, jnp.float32
    return pl.pallas_call(
        kernel,
        out_shape=jax.ShapeDtypeStruct(x.shape, bf16),
        in_specs=[anywhere] * 10,
        out_specs=pl.BlockSpec(memory_space=pltpu.VMEM),
        scratch_shapes=[
            pltpu.VMEM((4, 6, W, CH), bf16),
            pltpu.VMEM((4, 6, W, CH), bf16),
            pltpu.VMEM((6 * W, 4 * CH), bf16),
            pltpu.VMEM((2, 3, 3, 4 * CH, 2 * CH), bf16),
            pltpu.VMEM((3, 4 * W, 2 * CH), f32),
            pltpu.SMEM((64,), jnp.int32),
            pltpu.VMEM((6, 1, CH), f32),
            pltpu.VMEM((NX * NC, 1, CH), f32),
            pltpu.VMEM((NZ, 1, CH), f32),
            pltpu.VMEM((NY * NZ, 1, CH), f32),
            pltpu.VMEM((NX * NZ * NC * NY, 1, CH), f32),
            pltpu.VMEM((NZ * NX * NC, 1, CH), f32),
            pltpu.VMEM((NX * NZ * NC, 1, CH), f32),
            pltpu.SemaphoreType.DMA((8,)),
            pltpu.SemaphoreType.DMA((2, 18)),
            pltpu.SemaphoreType.DMA((2, 7)),
            pltpu.SemaphoreType.DMA((2, 7)),
            pltpu.SemaphoreType.DMA((5 + NZ * NC,)),
            pltpu.SemaphoreType.DMA((5 + NZ * NC,)),
            pltpu.SemaphoreType.REGULAR,
            pltpu.SemaphoreType.REGULAR,
        ],
        compiler_params=pltpu.CompilerParams(
            collective_id=0, has_side_effects=True, vmem_limit_bytes=48 * 1024 * 1024
        ),
        cost_estimate=pl.CostEstimate(
            flops=4 * 1024 * 27 * CH * CH, bytes_accessed=2500000, transcendentals=800000
        ),
    )(*operands)


def solution(mesh):
    placed = (P("clip", "slab", None, None), P(), P(), P(), P(), P(), P(), P(), P(), P())
    return jax.shard_map(
        per_device,
        mesh=mesh,
        in_specs=placed,
        out_specs=P("clip", "slab", None, None),
        check_vma=False,
    )
```

```python
import functools

import jax
import jax.numpy as jnp
from jax import lax
from jax.experimental import pallas as pl
from jax.experimental.pallas import tpu as pltpu
from jax.sharding import PartitionSpec as P

MESH = pl.DeviceIdType.MESH
NX, NZ, NC, NY = 4, 8, 2, 4
CH = 128
W = 128
EPS = 1e-06


def hops(dx, dz, dy):
    return min(dx, NX - dx) + min(dz, NZ - dz) + min(dy, NY - dy)


def offsets(nx, ny, nz, nc):
    every = [
        (dx, dy, dz, dc)
        for dx in range(nx) for dy in range(ny) for dz in range(nz) for dc in range(nc)
    ]
    return sorted(every[1:], key=lambda o: -hops(o[0], o[2], o[1]))


NEAR = offsets(NX, 1, 1, NC)
FAR = offsets(1, NY, NZ, 1)
EVERY = offsets(NX, NY, NZ, NC)
SIDE = [[o for o in EVERY if o[0] == dx] for dx in range(NX)]
BEYOND = sorted({o[2:] for o in SIDE[2]}, key=lambda o: -hops(2, o[0], 0))


def kernel(
    x_hbm, ids_hbm, g1, s1, k1, b1, g2, s2, k2, b2, out_ref,
    xbuf, hbuf, act, wts, pbuf, ids, vecs, near, parts, far, every, far_mask, mask,
    load_sem, w_sem, halo_send, halo_recv, st_send, st_recv, near_in, far_in,
):
    clip = lax.axis_index("clip")
    y = lax.axis_index("slab")
    cx = clip // (NZ * NC)
    cz = (clip // NC) % NZ
    cc = clip % NC
    clips = NX * NZ * NC

    def device(o):
        dx, dy, dz, dc = o
        at = (cx + dx) % NX if dx else cx
        at = at * NZ + ((cz + dz) % NZ if dz else cz)
        at = at * NC + ((cc + dc) % NC if dc else cc)
        return (at, (y + dy) % NY if dy else y)

    nxt, prv = (clip + 1) % clips, (clip + clips - 1) % clips
    up, down = (y + 1) % NY, (y + NY - 1) % NY

    barrier = pltpu.get_barrier_semaphore()

    def greet(dev):
        pl.semaphore_signal(barrier, inc=1, device_id=dev, device_id_type=MESH)

    def at(dx, dy, dz, core):
        chip = ((cx + dx) % NX) * NZ + (cz + dz) % NZ
        return (chip * NC + core, (y + dy) % NY)

    for dx in range(1, NX):
        greet(at(dx, 0, 0, 0))
    for side in (up, down):
        greet((clip - cc, side))

    @pl.when(cc == 0)
    def _():
        for side in (y, up, down):
            greet(((clip + clips - NC) % clips, side))
        greet((clip + 1, y))

    @pl.when(cc == 1)
    def _():
        greet((clip - 1, y))

    for _, dy, dz, _ in FAR:
        greet(at(0, dy, dz, 1))
    heard_near = 2 * (NX - 1) + 1 + 4 + 3
    heard_far = 2 * len(FAR) + 1

    loads = [pltpu.make_async_copy(x_hbm, xbuf.at[pl.ds(2, 2), pl.ds(1, 4)], load_sem.at[0])]
    loads.append(pltpu.make_async_copy(ids_hbm, ids, load_sem.at[1]))
    for n, v in enumerate((g1, s1, b1, g2, s2, b2)):
        loads.append(pltpu.make_async_copy(v, vecs.at[n], load_sem.at[2 + n]))
    for cp in loads:
        cp.start()
    w_loads = []
    for cv, k in enumerate((k1, k2)):
        for dt in range(3):
            for dx in range(3):
                for i in range(2):
                    j = dt + i
                    cp = pltpu.make_async_copy(
                        k.at[dt, :, dx],
                        wts.at[cv, dx, :, pl.ds(j * CH, CH), pl.ds(i * CH, CH)],
                        w_sem.at[cv, len(w_loads) % 18],
                    )
                    cp.start()
                    w_loads.append(cp)

    def stats_of(rows):
        s = jnp.zeros((8, CH), jnp.float32)
        q = jnp.zeros((8, CH), jnp.float32)
        for v in rows:
            v = v.reshape(W // 8, 8, CH)
            s = s + jnp.sum(v, axis=0)
            q = q + jnp.sum(v * v, axis=0)
        return s, q

    lane = lax.broadcasted_iota(jnp.int32, (1, CH), 1)
    even = lane % 2 == 0

    def packed(s, q):
        s = jnp.sum(s, axis=0, keepdims=True)
        q = jnp.sum(q, axis=0, keepdims=True)
        return jnp.where(even, s + pltpu.roll(s, CH - 1, 1), q + pltpu.roll(q, 1, 1))

    every[...] = jnp.zeros_like(every)
    loads[0].wait()
    s, q = stats_of(
        xbuf[2 + f, 1 + r].astype(jnp.float32) for f in range(2) for r in range(4)
    )
    me_near = cx * NC + cc
    me_far = y * NZ + cz
    me = clip * NY + y
    near[me_near] = packed(s, q)

    @pl.when(cc == 0)
    def _():
        pl.semaphore_wait(barrier, heard_near)
        pl.semaphore_signal(near_in, inc=1, device_id=(clip + 1, y), device_id_type=MESH)

    @pl.when(cc == 1)
    def _():
        pl.semaphore_wait(near_in, 1)

    def sends(offs, buf, at, n):
        return copies([(o, buf.at[at], buf.at[at]) for o in offs], n)

    def copies(plan, n):
        cps = []
        for o, src, dst in plan:
            cp = pltpu.make_async_remote_copy(
                src_ref=src, dst_ref=dst,
                send_sem=st_send.at[n], recv_sem=st_recv.at[n],
                device_id=device(o), device_id_type=MESH,
            )
            cp.start()
            cps.append(cp)
        return cps

    def halo(plan, n):
        return [
            pltpu.make_async_remote_copy(
                src_ref=src, dst_ref=dst, send_sem=halo_send.at[n, m],
                recv_sem=halo_recv.at[n, m], device_id=dev, device_id_type=MESH,
            )
            for m, (src, dst, dev) in plan
        ]

    def start(cps):
        for cp in cps:
            cp.start()

    frames = pl.ds(2, 2)
    carried = pl.ds(0, 2)

    def input_halo():
        own, top_row, low_row = xbuf.at[frames, pl.ds(1, 4)], xbuf.at[frames, 1], xbuf.at[frames, 4]
        plan = [
            (own, xbuf.at[carried, pl.ds(1, 4)], (nxt, y)),
            (low_row, xbuf.at[carried, 0], (nxt, up)),
            (top_row, xbuf.at[carried, 5], (nxt, down)),
            (low_row, xbuf.at[frames, 0], (clip, up)),
            (top_row, xbuf.at[frames, 5], (clip, down)),
        ]
        return halo(enumerate(plan), 0)

    def hidden_halo():
        plan = [
            (hbuf.at[frames, 1], hbuf.at[carried, 1], (nxt, y)),
            (hbuf.at[frames, 4], hbuf.at[carried, 4], (nxt, y)),
            (hbuf.at[frames, 1], hbuf.at[frames, 5], (clip, down)),
            (hbuf.at[frames, 4], hbuf.at[frames, 0], (clip, up)),
            (hbuf.at[frames, pl.ds(2, 2)], hbuf.at[carried, pl.ds(2, 2)], (nxt, y)),
            (hbuf.at[carried, 1], hbuf.at[carried, 5], (clip, down)),
            (hbuf.at[carried, 4], hbuf.at[carried, 0], (clip, up)),
        ]
        return halo(enumerate(plan), 1)

    def done(buf, count, sem):
        got = buf.at[pl.ds(0, count)]
        pltpu.make_async_copy(got, got, sem).wait()

    def arrived(buf, count, n):
        done(buf, count, st_recv.at[n])

    def reached(dz, dc):
        here = cz * NC + cc
        there = ((cz + dz) % NZ) * NC + (cc + dc) % NC
        return jnp.where(cx < 2, here - there, there - here) > 0

    sent = sends(NEAR, near, me_near, 0)
    halo_1 = input_halo()
    start(halo_1)

    for cp in loads[1:]:
        cp.wait()
    own_id = ids[clip]
    blocks = jnp.float32(0)
    for k in range(NX * NZ):
        for c in range(NC):
            m = jnp.where(ids[k * NC + c] == own_id, jnp.float32(1), jnp.float32(0))
            blocks = blocks + m
            m = jnp.full((1, CH), m, jnp.float32)
            mask[k * NC + c] = m
    column = [ids[(dx * NZ + cz) * NC + c] for dx in range(NX) for c in range(NC)]
    for k in range(NZ):
        target = ids[(cx * NZ + k) * NC + cc]
        for n, member in enumerate(column):
            m = jnp.where(member == target, jnp.float32(1), jnp.float32(0))
            far_mask[k * NX * NC + n] = jnp.full((1, CH), m, jnp.float32)
    prior_id = ids[jnp.maximum(clip - 1, 0)]
    same = jnp.where(prior_id == own_id, jnp.float32(1), jnp.float32(0))
    same = same * jnp.where(clip > 0, jnp.float32(1), jnp.float32(0))
    top = jnp.where(y > 0, jnp.float32(1), jnp.float32(0))
    bottom = jnp.where(y < NY - 1, jnp.float32(1), jnp.float32(0))
    one_count = 1.0 / (jnp.full((1, CH), blocks, jnp.float32) * (2 * 4 * NY * W * 4))
    zero = jnp.zeros((CH, CH), jnp.bfloat16)
    for cv in range(2):
        for dx in range(3):
            for dy in range(3):
                wts[cv, dx, dy, 0:CH, CH : 2 * CH] = zero
                wts[cv, dx, dy, 3 * CH : 4 * CH, 0:CH] = zero

    def finish(t, gain, shift):
        t = t + jnp.where(lane % 4 < 2, pltpu.roll(t, CH - 2, 1), pltpu.roll(t, 2, 1))
        t = t * one_count
        mean = jnp.where(even, t, pltpu.roll(t, 1, 1))
        square = jnp.where(even, pltpu.roll(t, CH - 1, 1), t)
        inverse = lax.rsqrt(square - mean * mean + EPS)
        scale = inverse * gain
        return 0.5 * scale, 0.5 * (shift - mean * scale)

    def tree(terms):
        while len(terms) > 1:
            terms = [sum(terms[k : k + 2][1:], terms[k]) for k in range(0, len(terms), 2)]
        return terms[0]

    def activate(buf, scale, offset, frames):
        for r in range(6):
            row = top if r == 0 else bottom if r == 5 else None
            for j in frames:
                keep = row
                if j < 2:
                    keep = same if row is None else same * row
                sc, of = (scale, offset) if keep is None else (scale * keep, offset * keep)
                h = buf[j, r].astype(jnp.float32) * sc + of
                v = h + h * jnp.tanh(h)
                act[r * W : (r + 1) * W, j * CH : (j + 1) * CH] = v.astype(jnp.bfloat16)

    def convolve(cv, rows, frames, more=False):
        k = slice(frames[0] * CH, (frames[-1] + 1) * CH)
        lhs = jnp.concatenate(
            [
                jnp.concatenate([act[(r + d) * W : (r + d + 1) * W, k] for r in rows], axis=0)
                for d in range(3)
            ],
            axis=1,
        )
        for dx in range(3):
            rhs = jnp.concatenate([wts[cv, dx, d, k, :] for d in range(3)], axis=0)
            p = jnp.dot(lhs, rhs, preferred_element_type=jnp.float32)
            for n, r in enumerate(rows):
                out = slice(r * W, (r + 1) * W)
                part = p[n * W : (n + 1) * W]
                pbuf[dx, out] = pbuf[dx, out] + part if more else part

    col = lax.broadcasted_iota(jnp.int32, (W, CH), 0)

    def joined(f, r, bias):
        at = (slice(r * W, (r + 1) * W), slice(f * CH, (f + 1) * CH))
        left = jnp.where(col == 0, 0.0, pltpu.roll(pbuf[(0, *at)], 1, 0))
        right = jnp.where(col == W - 1, 0.0, pltpu.roll(pbuf[(2, *at)], W - 1, 0))
        return (left + pbuf[(1, *at)]) + (right + bias)

    @pl.when(cc == 1)
    def _():
        pl.semaphore_wait(barrier, heard_far)
        pl.semaphore_signal(far_in, inc=1, device_id=(clip - 1, y), device_id_type=MESH)

    @pl.when(cc == 0)
    def _():
        pl.semaphore_wait(far_in, 1)

    arrived(near, len(NEAR), 0)
    for k in range(NZ):
        parts[k] = tree([near[n] * far_mask[k * NX * NC + n] for n in range(NX * NC)])
    far[me_far] = parts[cz]
    sent += copies([(o, parts.at[(cz + o[2]) % NZ], far.at[me_far]) for o in FAR], 1)
    for cp in w_loads:
        cp.wait()
    for cp in halo_1:
        cp.wait_recv()
    arrived(far, len(FAR), 1)
    t = tree([far[k] for k in range(NY * NZ)])
    scale, offset = finish(t, vecs[0], vecs[1])
    activate(xbuf, scale, offset, range(4))

    def hidden_rows(rows):
        for f in range(2):
            for r in rows:
                v = joined(f, r, vecs[2]).astype(jnp.bfloat16)
                hbuf[2 + f, 1 + r] = v
                yield v.astype(jnp.float32)

    convolve(0, (0, 3), range(4))
    s, q = stats_of(hidden_rows((0, 3)))
    halo_2 = hidden_halo()
    start(halo_2[:2])
    convolve(0, (1, 2), range(4))
    s2, q2 = stats_of(hidden_rows((1, 2)))
    s, q = s + s2, q + q2
    every[me] = packed(s, q)
    @pl.when(cx > 0)
    def _():
        sends(SIDE[3], every, me, 4)

    for dz, dc in BEYOND:

        @pl.when(reached(dz, dc))
        def _():
            sends([o for o in SIDE[2] if o[2:] == (dz, dc)], every, me, 5 + dz * NC + dc)

    sent += sends(SIDE[0], every, me, 2)
    @pl.when(cx < NX - 1)
    def _():
        sends(SIDE[1], every, me, 3)


    start(halo_2[4:5] + halo_2[2:4])
    for m in range(2):
        halo_2[m].wait_recv()
        halo_2[5 + m].start()
    arrived(every, len(SIDE[0]), 2)

    @pl.when(cx > 0)
    def _():
        arrived(every, len(SIDE[1]), 3)

    @pl.when(cx < NX - 1)
    def _():
        arrived(every, len(SIDE[3]), 4)

    for dz, dc in BEYOND:

        @pl.when(reached(-dz, dc))
        def _():
            arrived(every, NY, 5 + dz * NC + dc)

    t = tree(
        [
            tree([every[k * NY + n] for n in range(NY)]) * mask[k]
            for k in range(NX * NZ * NC)
        ]
    )
    scale, offset = finish(t, vecs[3], vecs[4])
    for m in (2, 3):
        halo_2[m].wait_recv()
    activate(hbuf, scale, offset, range(2, 4))
    convolve(1, range(4), range(2, 4))
    for m in (4, 5, 6):
        halo_2[m].wait_recv()
    activate(hbuf, scale, offset, range(2))
    convolve(1, range(4), range(2), more=True)
    for f in range(2):
        for r in range(4):
            v = joined(f, r, vecs[5]) + xbuf[2 + f, 1 + r].astype(jnp.float32)
            out_ref[f, r] = v.astype(jnp.bfloat16)
    for cp in sent + halo_1 + halo_2:
        cp.wait_send()

    @pl.when(cx < NX - 1)
    def _():
        done(every, len(SIDE[1]), st_send.at[3])

    @pl.when(cx > 0)
    def _():
        done(every, len(SIDE[3]), st_send.at[4])

    for dz, dc in BEYOND:

        @pl.when(reached(dz, dc))
        def _():
            done(every, NY, st_send.at[5 + dz * NC + dc])


def per_device(x, ids, g1, s1, k1, b1, g2, s2, k2, b2):
    vec = [v.reshape(1, CH) for v in (g1, s1, b1, g2, s2, b2)]
    g1, s1, b1, g2, s2, b2 = vec
    anywhere = pl.BlockSpec(memory_space=pl.ANY)
    operands = [
        pltpu.with_memory_space_constraint(v, pltpu.HBM)
        for v in (x, ids, g1, s1, k1, b1, g2, s2, k2, b2)
    ]
    bf16, f32 = jnp.bfloat16, jnp.float32
    return pl.pallas_call(
        kernel,
        out_shape=jax.ShapeDtypeStruct(x.shape, bf16),
        in_specs=[anywhere] * 10,
        out_specs=pl.BlockSpec(memory_space=pltpu.VMEM),
        scratch_shapes=[
            pltpu.VMEM((4, 6, W, CH), bf16),
            pltpu.VMEM((4, 6, W, CH), bf16),
            pltpu.VMEM((6 * W, 4 * CH), bf16),
            pltpu.VMEM((2, 3, 3, 4 * CH, 2 * CH), bf16),
            pltpu.VMEM((3, 4 * W, 2 * CH), f32),
            pltpu.SMEM((64,), jnp.int32),
            pltpu.VMEM((6, 1, CH), f32),
            pltpu.VMEM((NX * NC, 1, CH), f32),
            pltpu.VMEM((NZ, 1, CH), f32),
            pltpu.VMEM((NY * NZ, 1, CH), f32),
            pltpu.VMEM((NX * NZ * NC * NY, 1, CH), f32),
            pltpu.VMEM((NZ * NX * NC, 1, CH), f32),
            pltpu.VMEM((NX * NZ * NC, 1, CH), f32),
            pltpu.SemaphoreType.DMA((8,)),
            pltpu.SemaphoreType.DMA((2, 18)),
            pltpu.SemaphoreType.DMA((2, 7)),
            pltpu.SemaphoreType.DMA((2, 7)),
            pltpu.SemaphoreType.DMA((5 + NZ * NC,)),
            pltpu.SemaphoreType.DMA((5 + NZ * NC,)),
            pltpu.SemaphoreType.REGULAR,
            pltpu.SemaphoreType.REGULAR,
        ],
        compiler_params=pltpu.CompilerParams(
            collective_id=0, has_side_effects=True, vmem_limit_bytes=48 * 1024 * 1024
        ),
        cost_estimate=pl.CostEstimate(
            flops=4 * 1024 * 27 * CH * CH, bytes_accessed=2500000, transcendentals=800000
        ),
    )(*operands)


def solution(mesh):
    placed = (P("clip", "slab", None, None), P(), P(), P(), P(), P(), P(), P(), P(), P())
    return jax.shard_map(
        per_device,
        mesh=mesh,
        in_specs=placed,
        out_specs=P("clip", "slab", None, None),
        check_vma=False,
    )
```

```python
import functools

import jax
import jax.numpy as jnp
from jax import lax
from jax.experimental import pallas as pl
from jax.experimental.pallas import tpu as pltpu
from jax.sharding import PartitionSpec as P

MESH = pl.DeviceIdType.MESH
NX, NZ, NC, NY = 4, 8, 2, 4
CH = 128
W = 128
EPS = 1e-06


def hops(dx, dz, dy):
    return min(dx, NX - dx) + min(dz, NZ - dz) + min(dy, NY - dy)


def offsets(nx, ny, nz, nc):
    every = [
        (dx, dy, dz, dc)
        for dx in range(nx) for dy in range(ny) for dz in range(nz) for dc in range(nc)
    ]
    return sorted(every[1:], key=lambda o: -hops(o[0], o[2], o[1]))


NEAR = offsets(NX, 1, 1, NC)
FAR = offsets(1, NY, NZ, 1)
EVERY = offsets(NX, NY, NZ, NC)
SIDE = [[o for o in EVERY if o[0] == dx] for dx in range(NX)]
BEYOND = sorted({o[2:] for o in SIDE[2]}, key=lambda o: -hops(2, o[0], 0))


def kernel(
    x_hbm, ids_hbm, g1, s1, k1, b1, g2, s2, k2, b2, out_ref,
    xbuf, hbuf, act, wts, pbuf, ids, vecs, near, parts, far, every, far_mask, mask,
    load_sem, w_sem, halo_send, halo_recv, st_send, st_recv, near_in, far_in,
):
    clip = lax.axis_index("clip")
    y = lax.axis_index("slab")
    cx = clip // (NZ * NC)
    cz = (clip // NC) % NZ
    cc = clip % NC
    clips = NX * NZ * NC

    def device(o):
        dx, dy, dz, dc = o
        at = (cx + dx) % NX if dx else cx
        at = at * NZ + ((cz + dz) % NZ if dz else cz)
        at = at * NC + ((cc + dc) % NC if dc else cc)
        return (at, (y + dy) % NY if dy else y)

    nxt, prv = (clip + 1) % clips, (clip + clips - 1) % clips
    up, down = (y + 1) % NY, (y + NY - 1) % NY

    barrier = pltpu.get_barrier_semaphore()

    def greet(dev):
        pl.semaphore_signal(barrier, inc=1, device_id=dev, device_id_type=MESH)

    def at(dx, dy, dz, core):
        chip = ((cx + dx) % NX) * NZ + (cz + dz) % NZ
        return (chip * NC + core, (y + dy) % NY)

    for dx in range(1, NX):
        greet(at(dx, 0, 0, 0))
    for side in (up, down):
        greet((clip - cc, side))

    @pl.when(cc == 0)
    def _():
        for side in (y, up, down):
            greet(((clip + clips - NC) % clips, side))
        greet((clip + 1, y))

    @pl.when(cc == 1)
    def _():
        greet((clip - 1, y))

    for _, dy, dz, _ in FAR:
        greet(at(0, dy, dz, 1))
    heard_near = 2 * (NX - 1) + 1 + 4 + 3
    heard_far = 2 * len(FAR) + 1

    loads = [pltpu.make_async_copy(x_hbm, xbuf.at[pl.ds(2, 2), pl.ds(1, 4)], load_sem.at[0])]
    loads.append(pltpu.make_async_copy(ids_hbm, ids, load_sem.at[1]))
    for n, v in enumerate((g1, s1, b1, g2, s2, b2)):
        loads.append(pltpu.make_async_copy(v, vecs.at[n], load_sem.at[2 + n]))
    for cp in loads:
        cp.start()
    w_loads = []
    for cv, k in enumerate((k1, k2)):
        for dt in range(3):
            for dx in range(3):
                for i in range(2):
                    j = dt + i
                    cp = pltpu.make_async_copy(
                        k.at[dt, :, dx],
                        wts.at[cv, dx, :, pl.ds(j * CH, CH), pl.ds(i * CH, CH)],
                        w_sem.at[cv, len(w_loads) % 18],
                    )
                    cp.start()
                    w_loads.append(cp)

    def stats_of(rows):
        s = jnp.zeros((8, CH), jnp.float32)
        q = jnp.zeros((8, CH), jnp.float32)
        for v in rows:
            v = v.reshape(W // 8, 8, CH)
            s = s + jnp.sum(v, axis=0)
            q = q + jnp.sum(v * v, axis=0)
        return s, q

    lane = lax.broadcasted_iota(jnp.int32, (1, CH), 1)
    even = lane % 2 == 0

    def packed(s, q):
        s = jnp.sum(s, axis=0, keepdims=True)
        q = jnp.sum(q, axis=0, keepdims=True)
        return jnp.where(even, s + pltpu.roll(s, CH - 1, 1), q + pltpu.roll(q, 1, 1))

    every[...] = jnp.zeros_like(every)
    loads[0].wait()
    s, q = stats_of(
        xbuf[2 + f, 1 + r].astype(jnp.float32) for f in range(2) for r in range(4)
    )
    me_near = cx * NC + cc
    me_far = y * NZ + cz
    me = clip * NY + y
    near[me_near] = packed(s, q)

    @pl.when(cc == 0)
    def _():
        pl.semaphore_wait(barrier, heard_near)
        pl.semaphore_signal(near_in, inc=1, device_id=(clip + 1, y), device_id_type=MESH)

    @pl.when(cc == 1)
    def _():
        pl.semaphore_wait(near_in, 1)

    def sends(offs, buf, at, n):
        return copies([(o, buf.at[at], buf.at[at]) for o in offs], n)

    def copies(plan, n):
        cps = []
        for o, src, dst in plan:
            cp = pltpu.make_async_remote_copy(
                src_ref=src, dst_ref=dst,
                send_sem=st_send.at[n], recv_sem=st_recv.at[n],
                device_id=device(o), device_id_type=MESH,
            )
            cp.start()
            cps.append(cp)
        return cps

    def halo(plan, n):
        return [
            pltpu.make_async_remote_copy(
                src_ref=src, dst_ref=dst, send_sem=halo_send.at[n, m],
                recv_sem=halo_recv.at[n, m], device_id=dev, device_id_type=MESH,
            )
            for m, (src, dst, dev) in plan
        ]

    def start(cps):
        for cp in cps:
            cp.start()

    frames = pl.ds(2, 2)
    carried = pl.ds(0, 2)

    def input_halo():
        own, top_row, low_row = xbuf.at[frames, pl.ds(1, 4)], xbuf.at[frames, 1], xbuf.at[frames, 4]
        plan = [
            (own, xbuf.at[carried, pl.ds(1, 4)], (nxt, y)),
            (low_row, xbuf.at[carried, 0], (nxt, up)),
            (top_row, xbuf.at[carried, 5], (nxt, down)),
            (low_row, xbuf.at[frames, 0], (clip, up)),
            (top_row, xbuf.at[frames, 5], (clip, down)),
        ]
        return halo(enumerate(plan), 0)

    def hidden_halo():
        plan = [
            (hbuf.at[frames, 1], hbuf.at[carried, 1], (nxt, y)),
            (hbuf.at[frames, 4], hbuf.at[carried, 4], (nxt, y)),
            (hbuf.at[frames, 1], hbuf.at[frames, 5], (clip, down)),
            (hbuf.at[frames, 4], hbuf.at[frames, 0], (clip, up)),
            (hbuf.at[frames, pl.ds(2, 2)], hbuf.at[carried, pl.ds(2, 2)], (nxt, y)),
            (hbuf.at[carried, 1], hbuf.at[carried, 5], (clip, down)),
            (hbuf.at[carried, 4], hbuf.at[carried, 0], (clip, up)),
        ]
        return halo(enumerate(plan), 1)

    def done(buf, count, sem):
        got = buf.at[pl.ds(0, count)]
        pltpu.make_async_copy(got, got, sem).wait()

    def arrived(buf, count, n):
        done(buf, count, st_recv.at[n])

    def reached(dz, dc):
        here = cz * NC + cc
        there = ((cz + dz) % NZ) * NC + (cc + dc) % NC
        return jnp.where(cx < 2, here - there, there - here) > 0

    sent = sends(NEAR, near, me_near, 0)
    halo_1 = input_halo()
    start(halo_1)

    for cp in loads[1:]:
        cp.wait()
    own_id = ids[clip]
    blocks = jnp.float32(0)
    for k in range(NX * NZ):
        for c in range(NC):
            m = jnp.where(ids[k * NC + c] == own_id, jnp.float32(1), jnp.float32(0))
            blocks = blocks + m
            m = jnp.full((1, CH), m, jnp.float32)
            mask[k * NC + c] = m
    column = [ids[(dx * NZ + cz) * NC + c] for dx in range(NX) for c in range(NC)]
    for k in range(NZ):
        target = ids[(cx * NZ + k) * NC + cc]
        for n, member in enumerate(column):
            m = jnp.where(member == target, jnp.float32(1), jnp.float32(0))
            far_mask[k * NX * NC + n] = jnp.full((1, CH), m, jnp.float32)
    prior_id = ids[jnp.maximum(clip - 1, 0)]
    same = jnp.where(prior_id == own_id, jnp.float32(1), jnp.float32(0))
    same = same * jnp.where(clip > 0, jnp.float32(1), jnp.float32(0))
    top = jnp.where(y > 0, jnp.float32(1), jnp.float32(0))
    bottom = jnp.where(y < NY - 1, jnp.float32(1), jnp.float32(0))
    one_count = 1.0 / (jnp.full((1, CH), blocks, jnp.float32) * (2 * 4 * NY * W * 4))
    zero = jnp.zeros((CH, CH), jnp.bfloat16)
    for cv in range(2):
        for dx in range(3):
            for dy in range(3):
                wts[cv, dx, dy, 0:CH, CH : 2 * CH] = zero
                wts[cv, dx, dy, 3 * CH : 4 * CH, 0:CH] = zero

    def finish(t, gain, shift):
        t = t + jnp.where(lane % 4 < 2, pltpu.roll(t, CH - 2, 1), pltpu.roll(t, 2, 1))
        t = t * one_count
        mean = jnp.where(even, t, pltpu.roll(t, 1, 1))
        square = jnp.where(even, pltpu.roll(t, CH - 1, 1), t)
        inverse = lax.rsqrt(square - mean * mean + EPS)
        scale = inverse * gain
        return 0.5 * scale, 0.5 * (shift - mean * scale)

    def tree(terms):
        while len(terms) > 1:
            terms = [sum(terms[k : k + 2][1:], terms[k]) for k in range(0, len(terms), 2)]
        return terms[0]

    def activate(buf, scale, offset, frames):
        for r in range(6):
            row = top if r == 0 else bottom if r == 5 else None
            for j in frames:
                keep = row
                if j < 2:
                    keep = same if row is None else same * row
                sc, of = (scale, offset) if keep is None else (scale * keep, offset * keep)
                h = buf[j, r].astype(jnp.float32) * sc + of
                v = h + h * jnp.tanh(h)
                act[r * W : (r + 1) * W, j * CH : (j + 1) * CH] = v.astype(jnp.bfloat16)

    def convolve(cv, rows, frames, more=False):
        k = slice(frames[0] * CH, (frames[-1] + 1) * CH)
        lhs = jnp.concatenate(
            [
                jnp.concatenate([act[(r + d) * W : (r + d + 1) * W, k] for r in rows], axis=0)
                for d in range(3)
            ],
            axis=1,
        )
        for dx in range(3):
            rhs = jnp.concatenate([wts[cv, dx, d, k, :] for d in range(3)], axis=0)
            p = jnp.dot(lhs, rhs, preferred_element_type=jnp.float32)
            for n, r in enumerate(rows):
                out = slice(r * W, (r + 1) * W)
                part = p[n * W : (n + 1) * W]
                pbuf[dx, out] = pbuf[dx, out] + part if more else part

    col = lax.broadcasted_iota(jnp.int32, (W, CH), 0)

    def joined(f, r, bias):
        at = (slice(r * W, (r + 1) * W), slice(f * CH, (f + 1) * CH))
        left = jnp.where(col == 0, 0.0, pltpu.roll(pbuf[(0, *at)], 1, 0))
        right = jnp.where(col == W - 1, 0.0, pltpu.roll(pbuf[(2, *at)], W - 1, 0))
        return (left + pbuf[(1, *at)]) + (right + bias)

    @pl.when(cc == 1)
    def _():
        pl.semaphore_wait(barrier, heard_far)
        pl.semaphore_signal(far_in, inc=1, device_id=(clip - 1, y), device_id_type=MESH)

    @pl.when(cc == 0)
    def _():
        pl.semaphore_wait(far_in, 1)

    arrived(near, len(NEAR), 0)
    for k in range(NZ):
        parts[k] = tree([near[n] * far_mask[k * NX * NC + n] for n in range(NX * NC)])
    far[me_far] = parts[cz]
    sent += copies([(o, parts.at[(cz + o[2]) % NZ], far.at[me_far]) for o in FAR], 1)
    for cp in w_loads:
        cp.wait()
    for cp in halo_1:
        cp.wait_recv()
    arrived(far, len(FAR), 1)
    t = tree([far[k] for k in range(NY * NZ)])
    scale, offset = finish(t, vecs[0], vecs[1])
    activate(xbuf, scale, offset, range(4))

    def hidden_rows(rows):
        for f in range(2):
            for r in rows:
                v = joined(f, r, vecs[2]).astype(jnp.bfloat16)
                hbuf[2 + f, 1 + r] = v
                yield v.astype(jnp.float32)

    convolve(0, (0, 3), range(4))
    s, q = stats_of(hidden_rows((0, 3)))
    halo_2 = hidden_halo()
    start(halo_2[:2])
    convolve(0, (1, 2), range(4))
    s2, q2 = stats_of(hidden_rows((1, 2)))
    s, q = s + s2, q + q2
    every[me] = packed(s, q)
    @pl.when(cx > 0)
    def _():
        sends(SIDE[3], every, me, 4)

    for dz, dc in BEYOND:

        @pl.when(reached(dz, dc))
        def _():
            sends([o for o in SIDE[2] if o[2:] == (dz, dc)], every, me, 5 + dz * NC + dc)

    sent += sends(SIDE[0], every, me, 2)
    @pl.when(cx < NX - 1)
    def _():
        sends(SIDE[1], every, me, 3)


    start(halo_2[4:5] + halo_2[2:4])
    for m in range(2):
        halo_2[m].wait_recv()
        halo_2[5 + m].start()
    arrived(every, len(SIDE[0]), 2)

    @pl.when(cx > 0)
    def _():
        arrived(every, len(SIDE[1]), 3)

    @pl.when(cx < NX - 1)
    def _():
        arrived(every, len(SIDE[3]), 4)

    for dz, dc in BEYOND:

        @pl.when(reached(-dz, dc))
        def _():
            arrived(every, NY, 5 + dz * NC + dc)

    t = tree(
        [
            tree([every[k * NY + n] for n in range(NY)]) * mask[k]
            for k in range(NX * NZ * NC)
        ]
    )
    scale, offset = finish(t, vecs[3], vecs[4])
    for cp in halo_2[2:]:
        cp.wait_recv()
    activate(hbuf, scale, offset, range(4))
    convolve(1, range(4), range(4))
    for f in range(2):
        for r in range(4):
            v = joined(f, r, vecs[5]) + xbuf[2 + f, 1 + r].astype(jnp.float32)
            out_ref[f, r] = v.astype(jnp.bfloat16)
    for cp in sent + halo_1 + halo_2:
        cp.wait_send()

    @pl.when(cx < NX - 1)
    def _():
        done(every, len(SIDE[1]), st_send.at[3])

    @pl.when(cx > 0)
    def _():
        done(every, len(SIDE[3]), st_send.at[4])

    for dz, dc in BEYOND:

        @pl.when(reached(dz, dc))
        def _():
            done(every, NY, st_send.at[5 + dz * NC + dc])


def per_device(x, ids, g1, s1, k1, b1, g2, s2, k2, b2):
    vec = [v.reshape(1, CH) for v in (g1, s1, b1, g2, s2, b2)]
    g1, s1, b1, g2, s2, b2 = vec
    anywhere = pl.BlockSpec(memory_space=pl.ANY)
    operands = [
        pltpu.with_memory_space_constraint(v, pltpu.HBM)
        for v in (x, ids, g1, s1, k1, b1, g2, s2, k2, b2)
    ]
    bf16, f32 = jnp.bfloat16, jnp.float32
    return pl.pallas_call(
        kernel,
        out_shape=jax.ShapeDtypeStruct(x.shape, bf16),
        in_specs=[anywhere] * 10,
        out_specs=pl.BlockSpec(memory_space=pltpu.VMEM),
        scratch_shapes=[
            pltpu.VMEM((4, 6, W, CH), bf16),
            pltpu.VMEM((4, 6, W, CH), bf16),
            pltpu.VMEM((6 * W, 4 * CH), bf16),
            pltpu.VMEM((2, 3, 3, 4 * CH, 2 * CH), bf16),
            pltpu.VMEM((3, 4 * W, 2 * CH), f32),
            pltpu.SMEM((64,), jnp.int32),
            pltpu.VMEM((6, 1, CH), f32),
            pltpu.VMEM((NX * NC, 1, CH), f32),
            pltpu.VMEM((NZ, 1, CH), f32),
            pltpu.VMEM((NY * NZ, 1, CH), f32),
            pltpu.VMEM((NX * NZ * NC * NY, 1, CH), f32),
            pltpu.VMEM((NZ * NX * NC, 1, CH), f32),
            pltpu.VMEM((NX * NZ * NC, 1, CH), f32),
            pltpu.SemaphoreType.DMA((8,)),
            pltpu.SemaphoreType.DMA((2, 18)),
            pltpu.SemaphoreType.DMA((2, 7)),
            pltpu.SemaphoreType.DMA((2, 7)),
            pltpu.SemaphoreType.DMA((5 + NZ * NC,)),
            pltpu.SemaphoreType.DMA((5 + NZ * NC,)),
            pltpu.SemaphoreType.REGULAR,
            pltpu.SemaphoreType.REGULAR,
        ],
        compiler_params=pltpu.CompilerParams(
            collective_id=0, has_side_effects=True, vmem_limit_bytes=48 * 1024 * 1024
        ),
        cost_estimate=pl.CostEstimate(
            flops=4 * 1024 * 27 * CH * CH, bytes_accessed=2500000, transcendentals=800000
        ),
    )(*operands)


def solution(mesh):
    placed = (P("clip", "slab", None, None), P(), P(), P(), P(), P(), P(), P(), P(), P())
    return jax.shard_map(
        per_device,
        mesh=mesh,
        in_specs=placed,
        out_specs=P("clip", "slab", None, None),
        check_vma=False,
    )
```
